32 devices in a mesh: head: 4 (over y, x), blk: 8 (over z, core).
Axes of the slice: x: 2, y: 2, z: 4, core: 2. Of those that a mesh axis runs over, the one named last changes fastest.
Arguments:
- query: bfloat16 [4096, 2048], P(('blk', 'head')), may hold values from -8 to 8
- key_in: bfloat16 [4096, 2048], P(('blk', 'head')), may hold values from -8 to 8
- value: bfloat16 [4096, 2048], P(('blk', 'head')), may hold values from -6 to 6
- grad_out: bfloat16 [4096, 2048], P(('blk', 'head')), may hold values from -96 to 96
Outputs:
- grad_query: bfloat16 [4096, 2048], P(('blk', 'head'))
- grad_key: bfloat16 [4096, 2048], P(('blk', 'head'))
- grad_value: bfloat16 [4096, 2048], P(('blk', 'head'))
The draws below stay inside these ranges and needn't reach their ends.
All inputs are finite; a program needn't handle non-finite values.
Results may differ from the reference program's by a relative error of at most 0.0052.
Values may be sent and summed in bfloat16 or wider, within the bound.
No kernel may reach another device: no remote copies, remote signals or barrier semaphores. Data moves between devices by JAX's collectives and lax.ppermute only.
A program may use at most 64 MiB of HBM per device.

```python
import math
import jax
import jax.numpy as jnp
from jax import lax

HEADS = 16
HEAD_DIM = 128
D = 2048
HALF = 512
TILE = 512
SEQ = 4096


def query_key_pair(key):
    base_key = jax.random.fold_in(key, 1234)
    key_first, key_second, key_third, key_fourth = jax.random.split(base_key, 4)
    log_low = math.log(0.5)
    log_high = math.log(2.0)
    query_rows = jnp.exp(jax.random.uniform(key_third, (SEQ, 1), jnp.float32, log_low, log_high))
    key_rows = jnp.exp(jax.random.uniform(key_fourth, (SEQ, 1), jnp.float32, log_low, log_high))
    queries = jnp.clip(jax.random.normal(key_first, (SEQ, D), jnp.float32), -3.0, 3.0) * query_rows
    keys_all = jnp.clip(jax.random.normal(key_second, (SEQ, D), jnp.float32), -3.0, 3.0) * key_rows
    return (queries, keys_all)


def draw_query(key, part):
    return query_key_pair(key)[0].astype(jnp.bfloat16)


def draw_key_in(key, part):
    return query_key_pair(key)[1].astype(jnp.bfloat16)


def levels(stream_key, extent, cuts, smallest, top_value):
    loudness = 1.0
    for position, shards_of in cuts:
        steps = jax.random.uniform(jax.random.fold_in(jax.random.fold_in(stream_key, 6), position), (shards_of,), jnp.float32, smallest / len(cuts), top_value / len(cuts))
        loudness = loudness * jnp.repeat(jnp.exp(steps), extent[position] // shards_of).reshape((-1,) + (1,) * (len(extent) - 1 - position))
    return loudness


def centred(key, extent, scale, bound, cuts=(), held_as=jnp.bfloat16):
    values = scale * jax.random.normal(key, extent, jnp.float32)
    if cuts:
        values = values * levels(key, extent, cuts, -0.22, 0.18)
    return jnp.clip(values, -bound, bound).astype(held_as)


def setup_inputs(seed: int = 0) -> dict:
    key_of = jax.random.split(jax.random.key(seed), 5)
    query = draw_query(jax.random.fold_in(key_of[4], 71), 0)
    key_in = draw_key_in(jax.random.fold_in(key_of[4], 71), 0)
    value = centred(key_of[2], (SEQ, D), 1.0, 6.0, ((0, 32),))
    grad_out = centred(key_of[3], (SEQ, D), (max(1, HALF // 32)), 96.0, ((0, 32),))
    return dict(query=query, key_in=key_in, value=value, grad_out=grad_out)


def head_grads(operands):
    query_h, key_h, value_h, grad_h = operands
    score_scale = HEAD_DIM ** -0.5
    key_span = TILE + 2 * HALF
    padding = jnp.zeros((HALF, HEAD_DIM), key_h.dtype)
    key_pad = jnp.concatenate([padding, key_h, padding], axis=0)
    value_pad = jnp.concatenate([padding, value_h, padding], axis=0)
    row_ids = jnp.arange(TILE, dtype=jnp.int32)[:, None]
    col_ids = jnp.arange(key_span, dtype=jnp.int32)[None, :]

    def query_block(state, index):
        grad_key, grad_value = state
        offset = (index * TILE).astype(jnp.int32)
        query_part = lax.dynamic_slice_in_dim(query_h, offset, TILE, 0)
        grad_part = lax.dynamic_slice_in_dim(grad_h, offset, TILE, 0)
        key_part = lax.dynamic_slice_in_dim(key_pad, offset, key_span, 0)
        value_part = lax.dynamic_slice_in_dim(value_pad, offset, key_span, 0)
        key_pos = offset - HALF + col_ids
        query_pos = offset + row_ids
        within = (jnp.abs(query_pos - key_pos) <= HALF) & (key_pos >= 0) & (key_pos < SEQ)
        raw = jnp.dot(query_part, key_part.T, preferred_element_type=jnp.float32) * score_scale
        scores = jnp.where(within, raw, -1e30)
        row_max = jnp.max(scores, axis=1, keepdims=True)
        shifted = jnp.exp(scores - row_max)
        denominator = jnp.sum(shifted, axis=1, keepdims=True)
        output_rows = jnp.dot(shifted.astype(jnp.bfloat16), value_part, preferred_element_type=jnp.float32) / denominator
        log_total = row_max + jnp.log(denominator)
        row_delta = jnp.sum(grad_part.astype(jnp.float32) * output_rows, axis=1, keepdims=True)
        weights = jnp.exp(scores - log_total)
        grad_weights = jnp.dot(grad_part, value_part.T, preferred_element_type=jnp.float32)
        grad_scores = weights * (grad_weights - row_delta)
        weights_low = weights.astype(jnp.bfloat16)
        scores_low = grad_scores.astype(jnp.bfloat16)
        add_value = jnp.dot(weights_low.T, grad_part, preferred_element_type=jnp.float32)
        add_key = jnp.dot(scores_low.T, query_part, preferred_element_type=jnp.float32) * score_scale
        grad_query = jnp.dot(scores_low, key_part, preferred_element_type=jnp.float32) * score_scale
        old_key = lax.dynamic_slice_in_dim(grad_key, offset, key_span, 0)
        old_value = lax.dynamic_slice_in_dim(grad_value, offset, key_span, 0)
        grad_key = lax.dynamic_update_slice_in_dim(grad_key, old_key + add_key, offset, 0)
        grad_value = lax.dynamic_update_slice_in_dim(grad_value, old_value + add_value, offset, 0)
        return (grad_key, grad_value), grad_query

    zeros_f32 = jnp.zeros((SEQ + 2 * HALF, HEAD_DIM), jnp.float32)
    tile_ids = jnp.arange(SEQ // TILE, dtype=jnp.int32)
    (grad_key, grad_value), query_parts = lax.scan(query_block, (zeros_f32, zeros_f32), tile_ids)
    grad_query = query_parts.reshape(SEQ, HEAD_DIM)
    grad_key = grad_key[HALF:HALF + SEQ]
    grad_value = grad_value[HALF:HALF + SEQ]
    return grad_query.astype(jnp.bfloat16), grad_key.astype(jnp.bfloat16), grad_value.astype(jnp.bfloat16)


def by_head(matrix):
    return jnp.transpose(matrix.reshape(SEQ, HEADS, HEAD_DIM), (1, 0, 2))


def by_token(stacked):
    return jnp.transpose(stacked, (1, 0, 2)).reshape(SEQ, D)


def reference(query, key_in, value, grad_out):
    results = lax.map(head_grads, (by_head(query), by_head(key_in), by_head(value), by_head(grad_out)))
    return by_token(results[0]), by_token(results[1]), by_token(results[2])
```

```python
import functools
import math

import jax
import jax.numpy as jnp
from jax import lax
from jax.experimental import pallas as pl
from jax.experimental.pallas import tpu as pltpu
from jax.sharding import PartitionSpec as P

HEADS = 16
HEAD_DIM = 128
HALF = 512
TILE = 512
SUB = 256
SPAN = SUB + 2 * HALF
CHUNKS = SPAN // SUB
NEG = -1e30


def dot(a, b, contract):
    return lax.dot_general(
        a, b, ((contract[:1], contract[1:]), ((), ())), preferred_element_type=jnp.float32
    )


def attention_kernel(
    edge_ref, qd_ref, kv_ref, prev_ref, next_ref,
    dq_ref, own_ref, dprev_ref, dnext_ref,
    k_ext, v_ext, dk_ext, dv_ext, s_buf, p_buf,
):
    tile, tiles = pl.program_id(1), pl.num_programs(1)
    rows = kv_ref.shape[0] * kv_ref.shape[2]
    scale = HEAD_DIM ** -0.5
    rate = scale * math.log2(math.e)
    has_prev = jnp.logical_or(edge_ref[0] > 0, tile > 0)
    has_next = jnp.logical_or(edge_ref[1] > 0, tile < tiles - 1)

    @pl.when(tile == 0)
    def _():
        for which, ext in ((0, k_ext), (1, v_ext)):
            ext[:HALF] = prev_ref[:, which].reshape(HALF, HEAD_DIM)
            ext[HALF:HALF + rows] = kv_ref[:, which].reshape(rows, HEAD_DIM)
            ext[HALF + rows:] = next_ref[:, which].reshape(HALF, HEAD_DIM)
        dk_ext[...] = jnp.zeros_like(dk_ext)
        dv_ext[...] = jnp.zeros_like(dv_ext)

    query_all = qd_ref[:, 0].reshape(TILE, HEAD_DIM)
    grad_all = qd_ref[:, 1].reshape(TILE, HEAD_DIM)
    key_id = lax.broadcasted_iota(jnp.int32, (SUB, SUB), 0)
    query_id = lax.broadcasted_iota(jnp.int32, (SUB, SUB), 1)
    for sub in range(TILE // SUB):
        query = query_all[sub * SUB:(sub + 1) * SUB]
        grad = grad_all[sub * SUB:(sub + 1) * SUB]

        def ext_rows(c):
            start = tile * TILE + (sub + c) * SUB
            return pl.ds(pl.multiple_of(start, SUB), SUB)

        top = jnp.full((1, SUB), NEG, jnp.float32)
        for c in range(CHUNKS):
            s = dot(k_ext[ext_rows(c)], query, (1, 1)) * rate
            keep = None
            if c == 0:
                keep = key_id >= query_id
            if c == CHUNKS - 1:
                keep = key_id <= query_id
            if sub + c < HALF // SUB:
                keep = has_prev if keep is None else jnp.logical_and(keep, has_prev)
            if sub + c >= (HALF + TILE) // SUB:
                keep = has_next if keep is None else jnp.logical_and(keep, has_next)
            if keep is not None:
                s = jnp.where(keep, s, NEG)
            s_buf[c * SUB:(c + 1) * SUB] = s
            top = jnp.maximum(top, jnp.max(s, axis=0, keepdims=True))
        total = jnp.zeros((1, SUB), jnp.float32)
        delta = jnp.zeros((1, SUB), jnp.float32)
        for c in range(CHUNKS):
            at = slice(c * SUB, (c + 1) * SUB)
            e = jnp.exp2(s_buf[at] - top)
            dp = dot(v_ext[ext_rows(c)], grad, (1, 1))
            s_buf[at] = e
            p_buf[at] = dp
            total += jnp.sum(e, axis=0, keepdims=True)
            delta += jnp.sum(e * dp, axis=0, keepdims=True)
        inverse = 1.0 / total
        delta = delta * inverse
        dq = jnp.zeros((SUB, HEAD_DIM), jnp.float32)
        for c in range(CHUNKS):
            at = slice(c * SUB, (c + 1) * SUB)
            w = s_buf[at] * inverse
            ds = (w * (p_buf[at] - delta)).astype(jnp.bfloat16)
            dv_ext[ext_rows(c)] += dot(w.astype(jnp.bfloat16), grad, (1, 0))
            dk_ext[ext_rows(c)] += dot(ds, query, (1, 0))
            dq += dot(ds, k_ext[ext_rows(c)], (0, 0))
        per = SUB // dq_ref.shape[1]
        dq_ref[sub * per:(sub + 1) * per] = (
            (dq * scale).astype(jnp.bfloat16).reshape(per, dq_ref.shape[1], HEAD_DIM)
        )

    @pl.when(tile == tiles - 1)
    def _():
        for which, ext, factor in ((0, dk_ext, scale), (1, dv_ext, 1.0)):
            dprev_ref[:, which] = (
                (ext[:HALF] * factor).astype(jnp.bfloat16).reshape(dprev_ref[:, which].shape)
            )
            own_ref[:, which] = (ext[HALF:HALF + rows] * factor).reshape(own_ref[:, which].shape)
            dnext_ref[:, which] = (
                (ext[HALF + rows:] * factor).astype(jnp.bfloat16).reshape(dnext_ref[:, which].shape)
            )


def attention(edge, qd, kv, prev, nxt):
    n, _, r, width = kv.shape
    rows = n * r
    heads, tiles = width // HEAD_DIM, rows // TILE
    whole = pl.BlockSpec((n, 2, r, HEAD_DIM), lambda h, t, e: (0, 0, 0, h))
    halo = pl.BlockSpec((HALF // r, 2, r, HEAD_DIM), lambda h, t, e: (0, 0, 0, h))
    return pl.pallas_call(
        attention_kernel,
        grid_spec=pltpu.PrefetchScalarGridSpec(
            num_scalar_prefetch=1,
            grid=(heads, tiles),
            in_specs=[
                pl.BlockSpec((TILE // r, 2, r, HEAD_DIM), lambda h, t, e: (t, 0, 0, h)),
                whole, halo, halo,
            ],
            out_specs=[
                pl.BlockSpec((TILE // r, r, HEAD_DIM), lambda h, t, e: (t, 0, h)),
                whole, halo, halo,
            ],
            scratch_shapes=[
                pltpu.VMEM((rows + 2 * HALF, HEAD_DIM), jnp.bfloat16),
                pltpu.VMEM((rows + 2 * HALF, HEAD_DIM), jnp.bfloat16),
                pltpu.VMEM((rows + 2 * HALF, HEAD_DIM), jnp.float32),
                pltpu.VMEM((rows + 2 * HALF, HEAD_DIM), jnp.float32),
                pltpu.VMEM((SPAN, SUB), jnp.float32),
                pltpu.VMEM((SPAN, SUB), jnp.float32),
            ],
        ),
        out_shape=[
            jax.ShapeDtypeStruct((n, r, width), jnp.bfloat16),
            jax.ShapeDtypeStruct(kv.shape, jnp.float32),
            jax.ShapeDtypeStruct(prev.shape, jnp.bfloat16),
            jax.ShapeDtypeStruct(prev.shape, jnp.bfloat16),
        ],
        compiler_params=pltpu.CompilerParams(vmem_limit_bytes=40 * 1024 * 1024),
        name="attention",
    )(edge, qd, kv, prev, nxt)


def moved(array, by):
    count = lax.axis_size("blk")
    return lax.ppermute(array, "blk", [(i, i + by) for i in range(count) if 0 <= i + by < count])


def shards(query, key_in, value, grad_out):
    n = lax.axis_size("head")
    r = query.shape[0]
    width = query.shape[1] // n
    blocks = HALF // r

    def packed(a, b):
        return jnp.stack(
            [
                jnp.stack([x[:, i * width:(i + 1) * width] for x in (a, b)])
                for i in range(n)
            ]
        )

    def swapped(array):
        return lax.all_to_all(array, "head", split_axis=0, concat_axis=0, tiled=True)

    kv = swapped(packed(key_in, value))
    prev = moved(kv[n - blocks:], 1)
    nxt = moved(kv[:blocks], -1)
    qd = swapped(packed(query, grad_out))
    index = lax.axis_index("blk")
    edge = jnp.stack([index, lax.axis_size("blk") - 1 - index]).astype(jnp.int32)
    dq, own, dprev, dnext = attention(edge, qd, kv, prev, nxt)
    down = moved(dprev, -1).astype(jnp.float32)
    up = moved(dnext, 1).astype(jnp.float32)
    if n == blocks:
        total = own + down + up
    else:
        total = own.at[n - blocks:].add(down).at[:blocks].add(up)
    dkv = swapped(total.astype(jnp.bfloat16))
    dq = swapped(dq)

    def merged(x):
        return jnp.concatenate([x[i] for i in range(n)], axis=1)

    return merged(dq), merged(dkv[:, 0]), merged(dkv[:, 1])


def solution(mesh):
    spec = P(("blk", "head"), None)
    return jax.shard_map(
        shards, mesh=mesh, in_specs=(spec,) * 4, out_specs=(spec,) * 3, check_vma=False
    )
```

```python
import math

import jax
import jax.numpy as jnp
from jax import lax
from jax.experimental import pallas as pl
from jax.experimental.pallas import tpu as pltpu
from jax.sharding import PartitionSpec as P

HEADS = 16
HEAD_DIM = 128
HALF = 512
TILE = 512
SUB = 256
SPAN = SUB + 2 * HALF
CHUNKS = SPAN // SUB
NEG = -1e30
SCALE = HEAD_DIM ** -0.5
RATE = SCALE * math.log2(math.e)


def dot(a, b, contract):
    return lax.dot_general(
        a, b, ((contract[:1], contract[1:]), ((), ())), preferred_element_type=jnp.float32
    )


def rows_at(start, size):
    return pl.ds(pl.multiple_of(start, size), size)


def pack_kernel(order_ref, first_ref, second_ref, *outs):
    width = outs[0].shape[2]
    for k, out in enumerate(outs):
        columns = pl.ds(pl.multiple_of(order_ref[k] * width, 128), width)
        out[0] = first_ref[:, columns]
        out[1] = second_ref[:, columns]


def packed(order, first, second):
    n = order.shape[0]
    r, width = first.shape[0], first.shape[1] // n
    return pl.pallas_call(
        pack_kernel,
        in_specs=[pl.BlockSpec(memory_space=pltpu.SMEM)]
        + [pl.BlockSpec(memory_space=pltpu.VMEM)] * 2,
        out_specs=[pl.BlockSpec(memory_space=pltpu.VMEM)] * n,
        out_shape=[jax.ShapeDtypeStruct((2, r, width), first.dtype)] * n,
        name="pack",
    )(order, first, second)


def merge_kernel(order_ref, *refs):
    outs, ins = refs[-3:], refs[:-3]
    n = len(ins) // 2
    width = ins[0].shape[1]
    for k in range(n):
        columns = pl.ds(pl.multiple_of(order_ref[k] * width, 128), width)
        outs[0][:, columns] = ins[k][...]
        outs[1][:, columns] = ins[n + k][0]
        outs[2][:, columns] = ins[n + k][1]


def merged(order, dq, dkv):
    n = order.shape[0]
    r, width = dq[0].shape
    return pl.pallas_call(
        merge_kernel,
        in_specs=[pl.BlockSpec(memory_space=pltpu.SMEM)]
        + [pl.BlockSpec(memory_space=pltpu.VMEM)] * (2 * n),
        out_specs=[pl.BlockSpec(memory_space=pltpu.VMEM)] * 3,
        out_shape=[jax.ShapeDtypeStruct((r, n * width), dq[0].dtype)] * 3,
        name="merge",
    )(order, *dq, *dkv)


def query_kernel(n, order_ref, halo_ref, edge_ref, *refs):
    kv_refs, refs = refs[:n], refs[n:]
    qd_refs, refs = refs[:n], refs[n:]
    prev_ref, next_ref = refs[:2]
    dq_refs, refs = refs[2:2 + n], refs[2 + n:]
    stat_ref, part_ref, k_ext, v_ext, q_all, g_all, dq_all, s_buf, p_buf = refs
    tile, tiles = pl.program_id(1), pl.num_programs(1)
    r = kv_refs[0].shape[1]
    rows = n * r
    has_prev = jnp.logical_or(edge_ref[0] > 0, tile > 0)
    has_next = jnp.logical_or(edge_ref[1] > 0, tile < tiles - 1)
    single = rows == TILE

    @pl.when(tile == 0)
    def _():
        for i in range(HALF // r):
            at = halo_ref[i] * r
            for which, ext in ((0, k_ext), (1, v_ext)):
                ext[rows_at(at, r)] = prev_ref[i, which]
                ext[rows_at(HALF + rows + at, r)] = next_ref[i, which]
        for k in range(n):
            at = order_ref[k] * r
            for which, ext in ((0, k_ext), (1, v_ext)):
                ext[rows_at(HALF + at, r)] = kv_refs[k][which]
            q_all[rows_at(at, r)] = qd_refs[k][0]
            g_all[rows_at(at, r)] = qd_refs[k][1]
        if not single:
            part_ref[...] = jnp.zeros_like(part_ref)

    key_id = lax.broadcasted_iota(jnp.int32, (SUB, SUB), 0)
    query_id = lax.broadcasted_iota(jnp.int32, (SUB, SUB), 1)
    for sub in range(TILE // SUB):
        here = rows_at(tile * TILE + sub * SUB, SUB)
        query = q_all[here]
        grad = g_all[here]

        def ext_rows(c):
            return rows_at(tile * TILE + (sub + c) * SUB, SUB)

        top = jnp.full((1, SUB), NEG, jnp.float32)
        for c in range(CHUNKS):
            s = dot(k_ext[ext_rows(c)], query, (1, 1)) * RATE
            keep = None
            if c == 0:
                keep = key_id >= query_id
            if c == CHUNKS - 1:
                keep = key_id <= query_id
            if sub + c < HALF // SUB:
                keep = has_prev if keep is None else jnp.logical_and(keep, has_prev)
            if sub + c >= (HALF + TILE) // SUB:
                keep = has_next if keep is None else jnp.logical_and(keep, has_next)
            if keep is not None:
                s = jnp.where(keep, s, NEG)
            s_buf[c * SUB:(c + 1) * SUB] = s
            top = jnp.maximum(top, jnp.max(s, axis=0, keepdims=True))
        total = jnp.zeros((1, SUB), jnp.float32)
        delta = jnp.zeros((1, SUB), jnp.float32)
        for c in range(CHUNKS):
            at = slice(c * SUB, (c + 1) * SUB)
            e = jnp.exp2(s_buf[at] - top)
            dp = dot(v_ext[ext_rows(c)], grad, (1, 1))
            s_buf[at] = e
            p_buf[at] = dp
            total += jnp.sum(e, axis=0, keepdims=True)
            delta += jnp.sum(e * dp, axis=0, keepdims=True)
        inverse = 1.0 / total
        delta = delta * inverse
        stat_ref[0, 0:1, here] = top + jnp.log2(total)
        stat_ref[0, 1:2, here] = delta
        dq = jnp.zeros((SUB, HEAD_DIM), jnp.float32)
        for c in range(CHUNKS):
            at = slice(c * SUB, (c + 1) * SUB)
            w = s_buf[at] * inverse
            ds = (w * (p_buf[at] - delta)).astype(jnp.bfloat16)
            dq += dot(ds, k_ext[ext_rows(c)], (0, 0))
            low = w.astype(jnp.bfloat16)

            def keys_add(own, fresh):
                for which, left, right in ((0, ds, query), (1, low, grad)):
                    term = dot(left, right, (1, 0))
                    if fresh:
                        part_ref[which, own] = term
                    else:
                        part_ref[which, own] += term

            if single:
                e_at = (sub + c) * SUB - HALF
                if 0 <= e_at < TILE:
                    keys_add(slice(e_at, e_at + SUB), sub == 0)
            else:
                e_at = tile * TILE + (sub + c) * SUB - HALF

                @pl.when(jnp.logical_and(e_at >= 0, e_at < rows))
                def _():
                    keys_add(rows_at(e_at, SUB), False)
        dq_all[here] = (dq * SCALE).astype(jnp.bfloat16)

    @pl.when(tile == tiles - 1)
    def _():
        for k in range(n):
            dq_refs[k][...] = dq_all[rows_at(order_ref[k] * r, r)]


def query_part(order, halo, edge, kv, qd, prev, nxt):
    n = len(kv)
    _, r, width = kv[0].shape
    rows = n * r
    heads, tiles = width // HEAD_DIM, rows // TILE
    piece = pl.BlockSpec((2, r, HEAD_DIM), lambda h, t, *_: (0, 0, h))
    side = pl.BlockSpec((HALF // r, 2, r, HEAD_DIM), lambda h, t, *_: (0, 0, 0, h))
    outs = pl.pallas_call(
        lambda *refs: query_kernel(n, *refs),
        grid_spec=pltpu.PrefetchScalarGridSpec(
            num_scalar_prefetch=3,
            grid=(heads, tiles),
            in_specs=[piece] * (2 * n) + [side] * 2,
            out_specs=[pl.BlockSpec((r, HEAD_DIM), lambda h, t, *_: (0, h))] * n
            + [
                pl.BlockSpec((1, 2, rows), lambda h, t, *_: (h, 0, 0)),
                pl.BlockSpec((2, rows, HEAD_DIM), lambda h, t, *_: (0, 0, h)),
            ],
            scratch_shapes=[pltpu.VMEM((rows + 2 * HALF, HEAD_DIM), jnp.bfloat16)] * 2
            + [pltpu.VMEM((rows, HEAD_DIM), jnp.bfloat16)] * 3
            + [pltpu.VMEM((SPAN, SUB), jnp.float32)] * 2,
        ),
        out_shape=[jax.ShapeDtypeStruct((r, width), jnp.bfloat16)] * n
        + [
            jax.ShapeDtypeStruct((heads, 2, rows), jnp.float32),
            jax.ShapeDtypeStruct((2, rows, width), jnp.float32),
        ],
        compiler_params=pltpu.CompilerParams(vmem_limit_bytes=40 * 1024 * 1024),
        cost_estimate=pl.CostEstimate(
            flops=10 * heads * rows * SPAN * HEAD_DIM,
            bytes_accessed=12 * rows * width,
            transcendentals=heads * rows * SPAN,
        ),
        name="query_part",
    )(order, halo, edge, *kv, *qd, prev, nxt)
    return outs[:n], outs[n], outs[n + 1]


def key_kernel(n, order_ref, halo_ref, *refs):
    kv_refs, refs = refs[:n], refs[n:]
    sides, stats, part_ref = refs[:2], refs[2:4], refs[4]
    out_refs, (k_all, v_all, q_all, g_all, dk_all, dv_all) = refs[5:5 + n], refs[5 + n:]
    r = kv_refs[0].shape[1]
    rows = n * r
    for k in range(n):
        at = rows_at(order_ref[k] * r, r)
        k_all[at] = kv_refs[k][0]
        v_all[at] = kv_refs[k][1]
    for i in range(HALF // r):
        for side in range(2):
            at = rows_at(side * HALF + halo_ref[i] * r, r)
            q_all[at] = sides[side][i, 0]
            g_all[at] = sides[side][i, 1]
    dk_all[...] = part_ref[0]
    dv_all[...] = part_ref[1]
    key_id = lax.broadcasted_iota(jnp.int32, (SUB, SUB), 0)
    query_id = lax.broadcasted_iota(jnp.int32, (SUB, SUB), 1)
    steps = HALF // SUB
    for side in range(2):
        for b in range(steps):
            lanes = slice(b * SUB, (b + 1) * SUB)
            here = slice(side * HALF + b * SUB, side * HALF + (b + 1) * SUB)
            query = q_all[here]
            grad = g_all[here]
            log_total = stats[side][0, 0:1, lanes]
            delta = stats[side][0, 1:2, lanes]
            for a in range(steps):
                if (side == 0 and b < a) or (side == 1 and b > a):
                    continue
                first = a * SUB + (0 if side == 0 else rows - HALF)
                at = slice(first, first + SUB)
                w = jnp.exp2(dot(k_all[at], query, (1, 1)) * RATE - log_total)
                if a == b:
                    keep = key_id <= query_id if side == 0 else key_id >= query_id
                    w = jnp.where(keep, w, 0.0)
                ds = w * (dot(v_all[at], grad, (1, 1)) - delta)
                dk_all[at] += dot(ds.astype(jnp.bfloat16), query, (1, 0))
                dv_all[at] += dot(w.astype(jnp.bfloat16), grad, (1, 0))
    for k in range(n):
        at = rows_at(order_ref[k] * r, r)
        out_refs[k][0] = (dk_all[at] * SCALE).astype(jnp.bfloat16)
        out_refs[k][1] = dv_all[at].astype(jnp.bfloat16)


def key_part(order, halo, kv, prev, nxt, stat_prev, stat_next, part):
    n = len(kv)
    _, r, width = kv[0].shape
    rows = n * r
    heads = width // HEAD_DIM
    piece = pl.BlockSpec((2, r, HEAD_DIM), lambda h, *_: (0, 0, h))
    side = pl.BlockSpec((HALF // r, 2, r, HEAD_DIM), lambda h, *_: (0, 0, 0, h))
    stat = pl.BlockSpec((1, 2, HALF), lambda h, *_: (h, 0, 0))
    return pl.pallas_call(
        lambda *refs: key_kernel(n, *refs),
        grid_spec=pltpu.PrefetchScalarGridSpec(
            num_scalar_prefetch=2,
            grid=(heads,),
            in_specs=[piece] * n + [side] * 2 + [stat] * 2
            + [pl.BlockSpec((2, rows, HEAD_DIM), lambda h, *_: (0, 0, h))],
            out_specs=[piece] * n,
            scratch_shapes=[pltpu.VMEM((rows, HEAD_DIM), jnp.bfloat16)] * 2
            + [pltpu.VMEM((2 * HALF, HEAD_DIM), jnp.bfloat16)] * 2
            + [pltpu.VMEM((rows, HEAD_DIM), jnp.float32)] * 2,
        ),
        out_shape=[jax.ShapeDtypeStruct((2, r, width), jnp.bfloat16)] * n,
        compiler_params=pltpu.CompilerParams(vmem_limit_bytes=40 * 1024 * 1024),
        cost_estimate=pl.CostEstimate(
            flops=8 * heads * HALF * (HALF + SUB) * HEAD_DIM,
            bytes_accessed=24 * rows * width,
            transcendentals=heads * HALF * (HALF + SUB),
        ),
        name="key_part",
    )(order, halo, *kv, prev, nxt, stat_prev, stat_next, part)


def moved(array, by):
    count = lax.axis_size("blk")
    return lax.ppermute(array, "blk", [(i, i + by) for i in range(count) if 0 <= i + by < count])


def exchanged(pieces):
    n = len(pieces)
    return [pieces[0]] + [
        lax.ppermute(pieces[k], "head", [(i, i ^ k) for i in range(n)]) for k in range(1, n)
    ]


def shards(query, key_in, value, grad_out):
    n = lax.axis_size("head")
    blocks = HALF // query.shape[0]
    order = lax.axis_index("head").astype(jnp.int32) ^ jnp.arange(n, dtype=jnp.int32)
    index = lax.axis_index("blk")
    edge = jnp.stack([index, lax.axis_size("blk") - 1 - index]).astype(jnp.int32)

    def sides(pieces):
        stacked = jnp.stack(pieces)
        if n == blocks:
            return moved(stacked, 1), moved(stacked, -1)
        stacked = jnp.take(stacked, order, axis=0)
        return moved(stacked[n - blocks:], 1), moved(stacked[:blocks], -1)

    halo = order if n == blocks else jnp.arange(blocks, dtype=jnp.int32)
    kv = exchanged(packed(order, key_in, value))
    qd = exchanged(packed(order, query, grad_out))
    kv_prev, kv_next = sides(kv)
    qd_prev, qd_next = sides(qd)
    dq, stat, part = query_part(order, halo, edge, kv, qd, kv_prev, kv_next)
    stat_prev = moved(stat[:, :, -HALF:], 1)
    stat_next = moved(stat[:, :, :HALF], -1)
    dkv = key_part(order, halo, kv, qd_prev, qd_next, stat_prev, stat_next, part)
    dq, dkv = lax.optimization_barrier((exchanged(dq), dkv))
    return merged(order, dq, exchanged(dkv))


def solution(mesh):
    spec = P(("blk", "head"), None)
    return jax.shard_map(
        shards, mesh=mesh, in_specs=(spec,) * 4, out_specs=(spec,) * 3, check_vma=False
    )
```

```python
import math

import jax
import jax.numpy as jnp
from jax import lax
from jax.experimental import pallas as pl
from jax.experimental.pallas import tpu as pltpu
from jax.sharding import PartitionSpec as P

HEADS = 16
HEAD_DIM = 128
HALF = 512
TILE = 512
SUB = 256
SPAN = SUB + 2 * HALF
CHUNKS = SPAN // SUB
NEG = -1e30
STRIP = 64
SCALE = HEAD_DIM ** -0.5
RATE = SCALE * math.log2(math.e)
VMEM_BYTES = 24 * 1024 * 1024
SMALL_BYTES = 8 * 1024 * 1024


def dot(a, b, contract):
    return lax.dot_general(
        a, b, ((contract[:1], contract[1:]), ((), ())), preferred_element_type=jnp.float32
    )


def rows_at(start, size):
    return pl.ds(pl.multiple_of(start, size), size)


def pack_kernel(*refs):
    ins, outs, sems = refs[:2], refs[2:-1], refs[-1]
    n = len(outs)
    width = outs[0].shape[2]
    me = lax.axis_index("head")
    copies = []
    for k, out in enumerate(outs):
        columns = pl.ds(pl.multiple_of((me ^ k) * width, 128), width)
        for which in range(2):
            copies.append(
                pltpu.make_async_copy(ins[which].at[:, columns], out.at[which], sems.at[2 * k + which])
            )
    for copy in copies:
        copy.start()
    for copy in copies:
        copy.wait()


def packed(n, first, second):
    r, width = first.shape[0], first.shape[1] // n
    return pl.pallas_call(
        pack_kernel,
        in_specs=[pl.BlockSpec(memory_space=pl.ANY)] * 2,
        out_specs=[pl.BlockSpec(memory_space=pltpu.VMEM)] * n,
        out_shape=[jax.ShapeDtypeStruct((2, r, width), first.dtype)] * n,
        scratch_shapes=[pltpu.SemaphoreType.DMA((2 * n,))],
        compiler_params=pltpu.CompilerParams(vmem_limit_bytes=SMALL_BYTES),
        name="pack",
    )(first, second)


def merge_kernel(n, *refs):
    ins, outs, sems = refs[:n], refs[n:-1], refs[-1]
    width = ins[0].shape[-1]
    me = lax.axis_index("head")
    copies = []
    for k in range(n):
        columns = pl.ds(pl.multiple_of((me ^ k) * width, 128), width)
        for which, out in enumerate(outs):
            source = ins[k] if len(outs) == 1 else ins[k].at[which]
            copies.append(
                pltpu.make_async_copy(source, out.at[:, columns], sems.at[len(outs) * k + which])
            )
    for copy in copies:
        copy.start()
    for copy in copies:
        copy.wait()


def merged(pieces):
    n = len(pieces)
    r, width = pieces[0].shape[-2:]
    count = 1 if pieces[0].ndim == 2 else 2
    return pl.pallas_call(
        lambda *refs: merge_kernel(n, *refs),
        in_specs=[pl.BlockSpec(memory_space=pltpu.VMEM)] * n,
        out_specs=[pl.BlockSpec(memory_space=pl.ANY)] * count,
        out_shape=[jax.ShapeDtypeStruct((r, n * width), pieces[0].dtype)] * count,
        scratch_shapes=[pltpu.SemaphoreType.DMA((count * n,))],
        compiler_params=pltpu.CompilerParams(vmem_limit_bytes=SMALL_BYTES),
        name="merge",
    )(*pieces)


def ahead_by(turn_ref):
    return (
        lax.broadcasted_iota(jnp.int32, (SUB, SUB), 0)
        - lax.broadcasted_iota(jnp.int32, (SUB, SUB), 1)
    ) * turn_ref[0]


def query_kernel(n, place_ref, halo_ref, turn_ref, *refs):
    kv_refs, refs = refs[:n], refs[n:]
    qd_refs, refs = refs[:n], refs[n:]
    far_ref, near_ref = refs[:2]
    dq_refs, refs = refs[2:2 + n], refs[2 + n:]
    stat_ref, part_ref, give_ref, k_ext, v_ext, k_flip, q_all, g_all, dq_all = refs[:9]
    s_buf, p_buf, w_buf, d_buf = refs[9:13]
    r, width = kv_refs[0].shape[1:]
    rows = n * r
    tiles = rows // TILE
    ahead = ahead_by(turn_ref)

    def each_head(h, _):
        lanes = rows_at(h * HEAD_DIM, HEAD_DIM)
        for i in range(HALF // r):
            at = halo_ref[i] * r
            for which, ext in ((0, k_ext), (1, v_ext)):
                ext[rows_at(at, r)] = far_ref[i, which, :, lanes]
                ext[rows_at(HALF + rows + at, r)] = near_ref[i, which, :, lanes]
        for k in range(n):
            at = place_ref[k] * r
            for which, ext in ((0, k_ext), (1, v_ext)):
                ext[rows_at(HALF + at, r)] = kv_refs[k][which, :, lanes]
            q_all[rows_at(at, r)] = qd_refs[k][0, :, lanes]
            g_all[rows_at(at, r)] = qd_refs[k][1, :, lanes]
        k_flip[...] = k_ext[...].T
        if tiles > 1:
            refs[13][...] = jnp.zeros_like(refs[13])

        def each_tile(tile):
            first = tile * TILE
            has_far = turn_ref[1] > 0
            if tiles > 1:
                has_far = jnp.logical_or(has_far, tile > 0)

            def products(sub):
                here = rows_at(first + sub * SUB, SUB)
                query, grad = q_all[here], g_all[here]
                top = jnp.full((8, SUB), NEG, jnp.float32)
                for c in range(CHUNKS):
                    at = slice(c * SUB, (c + 1) * SUB)
                    keys = rows_at(first + (sub + c) * SUB, SUB)
                    s = dot(k_ext[keys], query, (1, 1)) * RATE
                    keep = None
                    if c == 0:
                        keep = ahead >= 0
                    if c == CHUNKS - 1:
                        keep = ahead <= 0
                    if sub + c < HALF // SUB:
                        keep = has_far if keep is None else jnp.logical_and(keep, has_far)
                    if keep is not None:
                        s = jnp.where(keep, s, NEG)
                    s_buf[sub, at] = s
                    top = jnp.maximum(top, jnp.max(s.reshape(SUB // 8, 8, SUB), axis=0))
                for c in range(CHUNKS):
                    at = slice(c * SUB, (c + 1) * SUB)
                    keys = rows_at(first + (sub + c) * SUB, SUB)
                    p_buf[sub, at] = dot(v_ext[keys], grad, (1, 1))
                return jnp.max(top, axis=0, keepdims=True)

            def softmax(sub, top):
                here = rows_at(first + sub * SUB, SUB)
                total = jnp.zeros((8, SUB), jnp.float32)
                delta = jnp.zeros((8, SUB), jnp.float32)
                for i in range(0, SPAN, STRIP):
                    at = slice(i, i + STRIP)
                    e = jnp.exp2(s_buf[sub, at] - top)
                    s_buf[sub, at] = e
                    total += jnp.sum(e.reshape(STRIP // 8, 8, SUB), axis=0)
                    delta += jnp.sum((e * p_buf[sub, at]).reshape(STRIP // 8, 8, SUB), axis=0)
                total = jnp.sum(total, axis=0, keepdims=True)
                inverse = 1.0 / total
                delta = jnp.sum(delta, axis=0, keepdims=True) * inverse
                stat_ref[h, 0:1, here] = top + jnp.log2(total)
                stat_ref[h, 1:2, here] = delta
                mine = slice(sub * SUB, (sub + 1) * SUB)
                for i in range(0, SPAN, STRIP):
                    at = slice(i, i + STRIP)
                    to = slice(sub * SUB + i, sub * SUB + i + STRIP)
                    w = s_buf[sub, at] * inverse
                    w_buf[to, mine] = w.astype(jnp.bfloat16)
                    d_buf[to, mine] = (w * (p_buf[sub, at] - delta)).astype(jnp.bfloat16)

            def query_grad(sub):
                mine = slice(sub * SUB, (sub + 1) * SUB)
                span = slice(sub * SUB, sub * SUB + SPAN)
                flip = k_flip[:, rows_at(first + sub * SUB, SPAN) if tiles > 1 else span]
                dq = dot(flip, d_buf[span, mine], (1, 0))
                here = rows_at(first + sub * SUB, SUB)
                dq_all[here] = (dq * SCALE).T.astype(jnp.bfloat16)

            tops = [products(sub) for sub in range(TILE // SUB)]
            for sub in range(TILE // SUB):
                softmax(sub, tops[sub])
                query_grad(sub)
            queries, grads = q_all[rows_at(first, TILE)], g_all[rows_at(first, TILE)]
            for which, buf, right in ((0, d_buf, queries), (1, w_buf, grads)):
                if tiles > 1:
                    acc = refs[13]
                    acc[which, rows_at(first, SUB)] += dot(buf[:SUB, :SUB], right[:SUB], (1, 0))
                    acc[which, rows_at(first + SUB, SPAN - SUB)] += dot(
                        buf[SUB:SPAN], right, (1, 0)
                    )
                    acc[which, rows_at(first + SPAN, SUB)] += dot(
                        buf[SPAN:, SUB:], right[SUB:], (1, 0)
                    )
                else:
                    part_ref[which, :, lanes] = dot(buf[HALF:HALF + TILE], right, (1, 0))
                    give_ref[which, :SUB, lanes] = dot(
                        buf[HALF + TILE:SPAN], right, (1, 0)
                    ).astype(jnp.bfloat16)
                    give_ref[which, SUB:, lanes] = dot(
                        buf[SPAN:, SUB:], right[SUB:], (1, 0)
                    ).astype(jnp.bfloat16)

        if tiles > 1:
            pl.loop(0, tiles)(each_tile)
            part_ref[:, :, lanes] = refs[13][:, HALF:HALF + rows]
            give_ref[:, :, lanes] = refs[13][:, HALF + rows:].astype(jnp.bfloat16)
        else:
            each_tile(0)
        for k in range(n):
            dq_refs[k][:, lanes] = dq_all[rows_at(place_ref[k] * r, r)]
        return 0

    lax.fori_loop(0, width // HEAD_DIM, each_head, 0)


def query_part(place, halo, turn, kv, qd, far, near):
    n = len(kv)
    _, r, width = kv[0].shape
    rows = n * r
    heads = width // HEAD_DIM
    ext = rows + 2 * HALF
    here, scalars = pl.BlockSpec(memory_space=pltpu.VMEM), pl.BlockSpec(memory_space=pltpu.SMEM)
    scratch = [
        pltpu.VMEM((ext, HEAD_DIM), jnp.bfloat16),
        pltpu.VMEM((ext, HEAD_DIM), jnp.bfloat16),
        pltpu.VMEM((HEAD_DIM, ext), jnp.bfloat16),
        pltpu.VMEM((rows, HEAD_DIM), jnp.bfloat16),
        pltpu.VMEM((rows, HEAD_DIM), jnp.bfloat16),
        pltpu.VMEM((rows, HEAD_DIM), jnp.bfloat16),
        pltpu.VMEM((TILE // SUB, SPAN, SUB), jnp.float32),
        pltpu.VMEM((TILE // SUB, SPAN, SUB), jnp.float32),
        pltpu.VMEM((TILE + 2 * HALF, TILE), jnp.bfloat16),
        pltpu.VMEM((TILE + 2 * HALF, TILE), jnp.bfloat16),
    ]
    if rows != TILE:
        scratch.append(pltpu.VMEM((2, ext, HEAD_DIM), jnp.float32))
    outs = pl.pallas_call(
        lambda *refs: query_kernel(n, *refs),
        in_specs=[scalars] * 3 + [here] * (2 * n + 2),
        out_specs=[here] * (n + 3),
        scratch_shapes=scratch,
        out_shape=[jax.ShapeDtypeStruct((r, width), jnp.bfloat16)] * n
        + [
            jax.ShapeDtypeStruct((heads, 2, rows), jnp.float32),
            jax.ShapeDtypeStruct((2, rows, width), jnp.float32),
            jax.ShapeDtypeStruct((2, HALF, width), jnp.bfloat16),
        ],
        compiler_params=pltpu.CompilerParams(vmem_limit_bytes=VMEM_BYTES),
        cost_estimate=pl.CostEstimate(
            flops=10 * heads * rows * SPAN * HEAD_DIM,
            bytes_accessed=12 * rows * width,
            transcendentals=heads * rows * SPAN,
        ),
        name="query_part",
    )(place, halo, turn, *kv, *qd, far, near)
    return outs[:n], outs[n], outs[n + 1], outs[n + 2]


def key_kernel(n, place_ref, halo_ref, turn_ref, *refs):
    kv_refs, refs = refs[:n], refs[n:]
    far_ref, stat_ref, part_ref, got_ref = refs[:4]
    out_refs, (k_all, v_all, q_all, g_all, acc, w_buf, d_buf) = refs[4:4 + n], refs[4 + n:]
    r, width = kv_refs[0].shape[1:]
    rows = n * r
    ahead = ahead_by(turn_ref)
    steps = HALF // SUB

    def each_head(h, _):
        lanes = rows_at(h * HEAD_DIM, HEAD_DIM)
        for k in range(n):
            at = rows_at(place_ref[k] * r, r)
            k_all[at] = kv_refs[k][0, :, lanes]
            v_all[at] = kv_refs[k][1, :, lanes]
        for i in range(HALF // r):
            at = rows_at(halo_ref[i] * r, r)
            q_all[at] = far_ref[i, 0, :, lanes]
            g_all[at] = far_ref[i, 1, :, lanes]
        acc[...] = part_ref[:, :, lanes]
        for a in range(steps):
            at = slice(rows - HALF + a * SUB, rows - HALF + (a + 1) * SUB)
            there = slice((steps - 1 - a) * SUB, (steps - a) * SUB)
            acc[:, at] += got_ref[:, there, lanes].astype(jnp.float32)
        for b in range(steps):
            here = slice(b * SUB, (b + 1) * SUB)
            there = slice((steps - 1 - b) * SUB, (steps - b) * SUB)
            query, grad = q_all[here], g_all[here]
            log_total = stat_ref[h, 0:1, there]
            delta = stat_ref[h, 1:2, there]
            for a in range(b + 1):
                at = slice(a * SUB, (a + 1) * SUB)
                w = jnp.exp2(dot(k_all[at], query, (1, 1)) * RATE - log_total)
                if a == b:
                    w = jnp.where(ahead <= 0, w, 0.0)
                w_buf[at, here] = w.astype(jnp.bfloat16)
                ds = w * (dot(v_all[at], grad, (1, 1)) - delta)
                d_buf[at, here] = ds.astype(jnp.bfloat16)
        for which, buf, right in ((0, d_buf, q_all), (1, w_buf, g_all)):
            for a in range(steps):
                at = slice(a * SUB, (a + 1) * SUB)
                acc[which, at] += dot(buf[at, a * SUB:], right[a * SUB:], (1, 0))
        for k in range(n):
            at = rows_at(place_ref[k] * r, r)
            out_refs[k][0, :, lanes] = (acc[0, at] * SCALE).astype(jnp.bfloat16)
            out_refs[k][1, :, lanes] = acc[1, at].astype(jnp.bfloat16)
        return 0

    lax.fori_loop(0, width // HEAD_DIM, each_head, 0)


def key_part(place, halo, turn, kv, far, stat, part, got):
    n = len(kv)
    _, r, width = kv[0].shape
    rows = n * r
    heads = width // HEAD_DIM
    here, scalars = pl.BlockSpec(memory_space=pltpu.VMEM), pl.BlockSpec(memory_space=pltpu.SMEM)
    return pl.pallas_call(
        lambda *refs: key_kernel(n, *refs),
        in_specs=[scalars] * 3 + [here] * (n + 4),
        out_specs=[here] * n,
        scratch_shapes=[
            pltpu.VMEM((rows, HEAD_DIM), jnp.bfloat16),
            pltpu.VMEM((rows, HEAD_DIM), jnp.bfloat16),
            pltpu.VMEM((HALF, HEAD_DIM), jnp.bfloat16),
            pltpu.VMEM((HALF, HEAD_DIM), jnp.bfloat16),
            pltpu.VMEM((2, rows, HEAD_DIM), jnp.float32),
            pltpu.VMEM((HALF, HALF), jnp.bfloat16),
            pltpu.VMEM((HALF, HALF), jnp.bfloat16),
        ],
        out_shape=[jax.ShapeDtypeStruct((2, r, width), jnp.bfloat16)] * n,
        compiler_params=pltpu.CompilerParams(vmem_limit_bytes=VMEM_BYTES),
        cost_estimate=pl.CostEstimate(
            flops=8 * heads * HALF * (HALF // 2 + SUB // 2) * HEAD_DIM,
            bytes_accessed=24 * rows * width,
            transcendentals=heads * HALF * (HALF // 2 + SUB // 2),
        ),
        name="key_part",
    )(place, halo, turn, *kv, far, stat, part, got)


def swapped(array, first):
    count = lax.axis_size("blk")
    pairs = [(i, i + 1) for i in range(first, count - 1, 2)]
    return lax.ppermute(array, "blk", pairs + [(j, i) for i, j in pairs])


def exchanged(pieces):
    n = len(pieces)
    return [pieces[0]] + [
        lax.ppermute(pieces[k], "head", [(i, i ^ k) for i in range(n)]) for k in range(1, n)
    ]


def shards(query, key_in, value, grad_out):
    n = lax.axis_size("head")
    blocks = HALF // query.shape[0]
    index = lax.axis_index("blk").astype(jnp.int32)
    odd = index & 1
    order = lax.axis_index("head").astype(jnp.int32) ^ jnp.arange(n, dtype=jnp.int32)
    place = order ^ (odd * (n - 2))
    if n == blocks:
        halo = place
    else:
        halo = jnp.arange(blocks, dtype=jnp.int32) ^ (blocks - 2)
    has_far = jnp.logical_and(index > 0, index < lax.axis_size("blk") - 1)
    turn = jnp.stack([1 - 2 * odd, has_far.astype(jnp.int32)])

    def edge(pieces, far):
        stacked = jnp.stack(pieces)
        if n == blocks:
            return stacked
        local = jnp.take(stacked, place, axis=0)
        return local[:blocks] if far else local[n - blocks:]

    kv_own = packed(n, key_in, value)
    qd_own = packed(n, query, grad_out)
    kv = exchanged(kv_own)
    qd = exchanged(qd_own)
    kv, qd_own = lax.optimization_barrier((kv, qd_own))
    kv_far = swapped(edge(kv, True), 1)
    kv_near = swapped(edge(kv, False), 0)
    qd_far = swapped(edge(qd, True), 1)
    dq, stat, part, give = query_part(place, halo, turn, kv, qd, kv_far, kv_near)
    stat_far = swapped(stat[:, :, :HALF], 1)
    got = swapped(give, 0)
    dkv = key_part(place, halo, turn, kv, qd_far, stat_far, part, got)
    dq, dkv = lax.optimization_barrier((exchanged(dq), dkv))
    return *merged(dq), *merged(exchanged(dkv))


def solution(mesh):
    spec = P(("blk", "head"), None)
    return jax.shard_map(
        shards, mesh=mesh, in_specs=(spec,) * 4, out_specs=(spec,) * 3, check_vma=False
    )
```

```python
import math

import jax
import jax.numpy as jnp
from jax import lax
from jax.experimental import pallas as pl
from jax.experimental.pallas import tpu as pltpu
from jax.sharding import PartitionSpec as P

HEADS = 16
HEAD_DIM = 128
HALF = 512
TILE = 512
SUB = 256
SPAN = SUB + 2 * HALF
CHUNKS = SPAN // SUB
NEG = -1e30
HINT = 30_000_000_000
STRIP = 64
SCALE = HEAD_DIM ** -0.5
RATE = SCALE * math.log2(math.e)
VMEM_BYTES = 24 * 1024 * 1024
SMALL_BYTES = 8 * 1024 * 1024


def dot(a, b, contract):
    return lax.dot_general(
        a, b, ((contract[:1], contract[1:]), ((), ())), preferred_element_type=jnp.float32
    )


def rows_at(start, size):
    return pl.ds(pl.multiple_of(start, size), size)


def pack_kernel(*refs):
    ins, outs, sems = refs[:2], refs[2:-1], refs[-1]
    n = len(outs)
    width = outs[0].shape[2]
    me = lax.axis_index("head")
    copies = []
    for k, out in enumerate(outs):
        columns = pl.ds(pl.multiple_of((me ^ k) * width, 128), width)
        for which in range(2):
            copies.append(
                pltpu.make_async_copy(ins[which].at[:, columns], out.at[which], sems.at[2 * k + which])
            )
    for copy in copies:
        copy.start()
    for copy in copies:
        copy.wait()


def packed(n, first, second):
    r, width = first.shape[0], first.shape[1] // n
    return pl.pallas_call(
        pack_kernel,
        in_specs=[pl.BlockSpec(memory_space=pltpu.HBM)] * 2,
        out_specs=[pl.BlockSpec(memory_space=pltpu.VMEM)] * n,
        out_shape=[jax.ShapeDtypeStruct((2, r, width), first.dtype)] * n,
        scratch_shapes=[pltpu.SemaphoreType.DMA((2 * n,))],
        compiler_params=pltpu.CompilerParams(vmem_limit_bytes=SMALL_BYTES),
        name="pack",
    )(first, second)


def stack_kernel(*refs):
    n = (len(refs) - 2)
    ins, out, sems = refs[:n], refs[n], refs[n + 1]
    copies = [pltpu.make_async_copy(ins[k], out.at[k], sems.at[k]) for k in range(n)]
    for copy in copies:
        copy.start()
    for copy in copies:
        copy.wait()


def stacked(pieces, flops=0):
    n = len(pieces)
    return pl.pallas_call(
        stack_kernel,
        in_specs=[pl.BlockSpec(memory_space=pltpu.VMEM)] * n,
        out_specs=pl.BlockSpec(memory_space=pltpu.VMEM),
        out_shape=jax.ShapeDtypeStruct((n, *pieces[0].shape), pieces[0].dtype),
        scratch_shapes=[pltpu.SemaphoreType.DMA((n,))],
        compiler_params=pltpu.CompilerParams(vmem_limit_bytes=SMALL_BYTES),
        cost_estimate=pl.CostEstimate(flops=flops, bytes_accessed=0, transcendentals=0),
        name="stack",
    )(*pieces)


def merge_kernel(n, *refs):
    ins, outs, sems = refs[:n], refs[n:-1], refs[-1]
    width = ins[0].shape[-1]
    me = lax.axis_index("head")
    copies = []
    for k in range(n):
        columns = pl.ds(pl.multiple_of((me ^ k) * width, 128), width)
        for which, out in enumerate(outs):
            source = ins[k] if len(outs) == 1 else ins[k].at[which]
            copies.append(
                pltpu.make_async_copy(source, out.at[:, columns], sems.at[len(outs) * k + which])
            )
    for copy in copies:
        copy.start()
    for copy in copies:
        copy.wait()


def merged(pieces):
    n = len(pieces)
    r, width = pieces[0].shape[-2:]
    count = 1 if pieces[0].ndim == 2 else 2
    return pl.pallas_call(
        lambda *refs: merge_kernel(n, *refs),
        in_specs=[pl.BlockSpec(memory_space=pltpu.VMEM)] * n,
        out_specs=[pl.BlockSpec(memory_space=pl.ANY)] * count,
        out_shape=[jax.ShapeDtypeStruct((r, n * width), pieces[0].dtype)] * count,
        scratch_shapes=[pltpu.SemaphoreType.DMA((count * n,))],
        compiler_params=pltpu.CompilerParams(vmem_limit_bytes=SMALL_BYTES),
        name="merge",
    )(*pieces)


def ahead_by(turn_ref):
    return (
        lax.broadcasted_iota(jnp.int32, (SUB, SUB), 0)
        - lax.broadcasted_iota(jnp.int32, (SUB, SUB), 1)
    ) * turn_ref[0]


def members(refs):
    return [ref.at[i] for ref in refs for i in range(ref.shape[0])]


def query_kernel(n, groups, place_ref, halo_ref, turn_ref, *refs):
    kv_refs, refs = refs[:n], refs[n:]
    qd_ref, refs = refs[0], refs[1:]
    far_refs, near_refs, refs = refs[:groups], refs[groups:2 * groups], refs[2 * groups:]
    dq_refs, refs = refs[:n], refs[n:]
    stat_ref, part_ref, give_ref, k_ext, v_ext, k_flip, q_all, g_all, dq_all = refs[:9]
    s_buf, p_buf, w_buf, d_buf = refs[9:13]
    r, width = kv_refs[0].shape[1:]
    rows = n * r
    tiles = rows // TILE
    ahead = ahead_by(turn_ref)

    def each_head(h, _):
        lanes = rows_at(h * HEAD_DIM, HEAD_DIM)
        for i, (far, near) in enumerate(zip(members(far_refs), members(near_refs))):
            at = halo_ref[i] * r
            for which, ext in ((0, k_ext), (1, v_ext)):
                ext[rows_at(at, r)] = far[which, :, lanes]
                ext[rows_at(HALF + rows + at, r)] = near[which, :, lanes]
        for k in range(n):
            at = place_ref[k] * r
            for which, ext in ((0, k_ext), (1, v_ext)):
                ext[rows_at(HALF + at, r)] = kv_refs[k][which, :, lanes]
            q_all[rows_at(at, r)] = qd_ref[k, 0, :, lanes]
            g_all[rows_at(at, r)] = qd_ref[k, 1, :, lanes]
        k_flip[...] = k_ext[...].T
        if tiles > 1:
            refs[13][...] = jnp.zeros_like(refs[13])

        def each_tile(tile):
            first = tile * TILE
            has_far = turn_ref[1] > 0
            if tiles > 1:
                has_far = jnp.logical_or(has_far, tile > 0)

            def products(sub):
                here = rows_at(first + sub * SUB, SUB)
                query, grad = q_all[here], g_all[here]
                top = jnp.full((8, SUB), NEG, jnp.float32)
                for c in range(CHUNKS):
                    at = slice(c * SUB, (c + 1) * SUB)
                    keys = rows_at(first + (sub + c) * SUB, SUB)
                    s = dot(k_ext[keys], query, (1, 1)) * RATE
                    keep = None
                    if c == 0:
                        keep = ahead >= 0
                    if c == CHUNKS - 1:
                        keep = ahead <= 0
                    if sub + c < HALF // SUB:
                        keep = has_far if keep is None else jnp.logical_and(keep, has_far)
                    if keep is not None:
                        s = jnp.where(keep, s, NEG)
                    s_buf[sub, at] = s
                    top = jnp.maximum(top, jnp.max(s.reshape(SUB // 8, 8, SUB), axis=0))
                for c in range(CHUNKS):
                    at = slice(c * SUB, (c + 1) * SUB)
                    keys = rows_at(first + (sub + c) * SUB, SUB)
                    p_buf[sub, at] = dot(v_ext[keys], grad, (1, 1))
                return jnp.max(top, axis=0, keepdims=True)

            def softmax(sub, top):
                here = rows_at(first + sub * SUB, SUB)
                total = jnp.zeros((8, SUB), jnp.float32)
                delta = jnp.zeros((8, SUB), jnp.float32)
                for i in range(0, SPAN, STRIP):
                    at = slice(i, i + STRIP)
                    e = jnp.exp2(s_buf[sub, at] - top)
                    s_buf[sub, at] = e
                    total += jnp.sum(e.reshape(STRIP // 8, 8, SUB), axis=0)
                    delta += jnp.sum((e * p_buf[sub, at]).reshape(STRIP // 8, 8, SUB), axis=0)
                total = jnp.sum(total, axis=0, keepdims=True)
                inverse = 1.0 / total
                delta = jnp.sum(delta, axis=0, keepdims=True) * inverse
                stat_ref[h, 0:1, here] = top + jnp.log2(total)
                stat_ref[h, 1:2, here] = delta
                mine = slice(sub * SUB, (sub + 1) * SUB)
                for i in range(0, SPAN, STRIP):
                    at = slice(i, i + STRIP)
                    to = slice(sub * SUB + i, sub * SUB + i + STRIP)
                    w = s_buf[sub, at] * inverse
                    w_buf[to, mine] = w.astype(jnp.bfloat16)
                    d_buf[to, mine] = (w * (p_buf[sub, at] - delta)).astype(jnp.bfloat16)

            def query_grad(sub):
                mine = slice(sub * SUB, (sub + 1) * SUB)
                span = slice(sub * SUB, sub * SUB + SPAN)
                flip = k_flip[:, rows_at(first + sub * SUB, SPAN) if tiles > 1 else span]
                dq = dot(flip, d_buf[span, mine], (1, 0))
                here = rows_at(first + sub * SUB, SUB)
                dq_all[here] = (dq * SCALE).T.astype(jnp.bfloat16)

            tops = [products(sub) for sub in range(TILE // SUB)]
            for sub in range(TILE // SUB):
                softmax(sub, tops[sub])
                query_grad(sub)
            queries, grads = q_all[rows_at(first, TILE)], g_all[rows_at(first, TILE)]
            for which, buf, right in ((0, d_buf, queries), (1, w_buf, grads)):
                if tiles > 1:
                    acc = refs[13]
                    acc[which, rows_at(first, SUB)] += dot(buf[:SUB, :SUB], right[:SUB], (1, 0))
                    acc[which, rows_at(first + SUB, SPAN - SUB)] += dot(
                        buf[SUB:SPAN], right, (1, 0)
                    )
                    acc[which, rows_at(first + SPAN, SUB)] += dot(
                        buf[SPAN:, SUB:], right[SUB:], (1, 0)
                    )
                else:
                    part_ref[which, :, lanes] = dot(buf[HALF:HALF + TILE], right, (1, 0))
                    give_ref[which, :SUB, lanes] = dot(
                        buf[HALF + TILE:SPAN], right, (1, 0)
                    ).astype(jnp.bfloat16)
                    give_ref[which, SUB:, lanes] = dot(
                        buf[SPAN:, SUB:], right[SUB:], (1, 0)
                    ).astype(jnp.bfloat16)

        if tiles > 1:
            pl.loop(0, tiles)(each_tile)
            part_ref[:, :, lanes] = refs[13][:, HALF:HALF + rows]
            give_ref[:, :, lanes] = refs[13][:, HALF + rows:].astype(jnp.bfloat16)
        else:
            each_tile(0)
        for k in range(n):
            dq_refs[k][:, lanes] = dq_all[rows_at(place_ref[k] * r, r)]
        return 0

    lax.fori_loop(0, width // HEAD_DIM, each_head, 0)


def query_part(place, halo, turn, kv, qd, far, near):
    n = len(kv)
    _, r, width = kv[0].shape
    rows = n * r
    heads = width // HEAD_DIM
    ext = rows + 2 * HALF
    here, scalars = pl.BlockSpec(memory_space=pltpu.VMEM), pl.BlockSpec(memory_space=pltpu.SMEM)
    scratch = [
        pltpu.VMEM((ext, HEAD_DIM), jnp.bfloat16),
        pltpu.VMEM((ext, HEAD_DIM), jnp.bfloat16),
        pltpu.VMEM((HEAD_DIM, ext), jnp.bfloat16),
        pltpu.VMEM((rows, HEAD_DIM), jnp.bfloat16),
        pltpu.VMEM((rows, HEAD_DIM), jnp.bfloat16),
        pltpu.VMEM((rows, HEAD_DIM), jnp.bfloat16),
        pltpu.VMEM((TILE // SUB, SPAN, SUB), jnp.float32),
        pltpu.VMEM((TILE // SUB, SPAN, SUB), jnp.float32),
        pltpu.VMEM((TILE + 2 * HALF, TILE), jnp.bfloat16),
        pltpu.VMEM((TILE + 2 * HALF, TILE), jnp.bfloat16),
    ]
    if rows != TILE:
        scratch.append(pltpu.VMEM((2, ext, HEAD_DIM), jnp.float32))
    outs = pl.pallas_call(
        lambda *refs: query_kernel(n, len(far), *refs),
        in_specs=[scalars] * 3 + [here] * (n + 1 + 2 * len(far)),
        out_specs=[here] * (n + 3),
        scratch_shapes=scratch,
        out_shape=[jax.ShapeDtypeStruct((r, width), jnp.bfloat16)] * n
        + [
            jax.ShapeDtypeStruct((heads, 2, rows), jnp.float32),
            jax.ShapeDtypeStruct((2, rows, width), jnp.float32),
            jax.ShapeDtypeStruct((2, HALF, width), jnp.bfloat16),
        ],
        compiler_params=pltpu.CompilerParams(vmem_limit_bytes=VMEM_BYTES),
        cost_estimate=pl.CostEstimate(
            flops=10 * heads * rows * SPAN * HEAD_DIM,
            bytes_accessed=12 * rows * width,
            transcendentals=heads * rows * SPAN,
        ),
        name="query_part",
    )(place, halo, turn, *kv, qd, *far, *near)
    return outs[:n], outs[n], outs[n + 1], outs[n + 2]


def key_kernel(n, place_ref, halo_ref, turn_ref, *refs):
    kv_refs, refs = refs[:n], refs[n:]
    far_ref, stat_ref, part_ref, got_ref = refs[:4]
    out_refs, (k_all, v_all, q_all, g_all, acc, w_buf, d_buf) = refs[4:4 + n], refs[4 + n:]
    r, width = kv_refs[0].shape[1:]
    rows = n * r
    ahead = ahead_by(turn_ref)
    steps = HALF // SUB

    def each_head(h, _):
        lanes = rows_at(h * HEAD_DIM, HEAD_DIM)
        for k in range(n):
            at = rows_at(place_ref[k] * r, r)
            k_all[at] = kv_refs[k][0, :, lanes]
            v_all[at] = kv_refs[k][1, :, lanes]
        for i in range(HALF // r):
            at = rows_at(halo_ref[i] * r, r)
            q_all[at] = far_ref[i, 0, :, lanes]
            g_all[at] = far_ref[i, 1, :, lanes]
        acc[...] = part_ref[:, :, lanes]
        for a in range(steps):
            at = slice(rows - HALF + a * SUB, rows - HALF + (a + 1) * SUB)
            there = slice((steps - 1 - a) * SUB, (steps - a) * SUB)
            acc[:, at] += got_ref[:, there, lanes].astype(jnp.float32)
        for b in range(steps):
            here = slice(b * SUB, (b + 1) * SUB)
            there = slice((steps - 1 - b) * SUB, (steps - b) * SUB)
            query, grad = q_all[here], g_all[here]
            log_total = stat_ref[h, 0:1, there]
            delta = stat_ref[h, 1:2, there]
            for a in range(b + 1):
                at = slice(a * SUB, (a + 1) * SUB)
                w = jnp.exp2(dot(k_all[at], query, (1, 1)) * RATE - log_total)
                if a == b:
                    w = jnp.where(ahead <= 0, w, 0.0)
                w_buf[at, here] = w.astype(jnp.bfloat16)
                ds = w * (dot(v_all[at], grad, (1, 1)) - delta)
                d_buf[at, here] = ds.astype(jnp.bfloat16)
        for which, buf, right in ((0, d_buf, q_all), (1, w_buf, g_all)):
            for a in range(steps):
                at = slice(a * SUB, (a + 1) * SUB)
                acc[which, at] += dot(buf[at, a * SUB:], right[a * SUB:], (1, 0))
        for k in range(n):
            at = rows_at(place_ref[k] * r, r)
            out_refs[k][0, :, lanes] = (acc[0, at] * SCALE).astype(jnp.bfloat16)
            out_refs[k][1, :, lanes] = acc[1, at].astype(jnp.bfloat16)
        return 0

    lax.fori_loop(0, width // HEAD_DIM, each_head, 0)


def key_part(place, halo, turn, kv, far, stat, part, got):
    n = len(kv)
    _, r, width = kv[0].shape
    rows = n * r
    heads = width // HEAD_DIM
    here, scalars = pl.BlockSpec(memory_space=pltpu.VMEM), pl.BlockSpec(memory_space=pltpu.SMEM)
    return pl.pallas_call(
        lambda *refs: key_kernel(n, *refs),
        in_specs=[scalars] * 3 + [here] * (n + 4),
        out_specs=[here] * n,
        scratch_shapes=[
            pltpu.VMEM((rows, HEAD_DIM), jnp.bfloat16),
            pltpu.VMEM((rows, HEAD_DIM), jnp.bfloat16),
            pltpu.VMEM((HALF, HEAD_DIM), jnp.bfloat16),
            pltpu.VMEM((HALF, HEAD_DIM), jnp.bfloat16),
            pltpu.VMEM((2, rows, HEAD_DIM), jnp.float32),
            pltpu.VMEM((HALF, HALF), jnp.bfloat16),
            pltpu.VMEM((HALF, HALF), jnp.bfloat16),
        ],
        out_shape=[jax.ShapeDtypeStruct((2, r, width), jnp.bfloat16)] * n,
        compiler_params=pltpu.CompilerParams(vmem_limit_bytes=VMEM_BYTES),
        cost_estimate=pl.CostEstimate(
            flops=8 * heads * HALF * (HALF // 2 + SUB // 2) * HEAD_DIM,
            bytes_accessed=24 * rows * width,
            transcendentals=heads * HALF * (HALF // 2 + SUB // 2),
        ),
        name="key_part",
    )(place, halo, turn, *kv, far, stat, part, got)


def swapped(array, first):
    count = lax.axis_size("blk")
    pairs = [(i, i + 1) for i in range(first, count - 1, 2)]
    return lax.ppermute(array, "blk", pairs + [(j, i) for i, j in pairs])


def exchanged(pieces):
    n = len(pieces)
    return [pieces[0]] + [
        lax.ppermute(pieces[k], "head", [(i, i ^ k) for i in range(n)]) for k in range(1, n)
    ]


def shards(query, key_in, value, grad_out):
    n = lax.axis_size("head")
    blocks = HALF // query.shape[0]
    index = lax.axis_index("blk").astype(jnp.int32)
    odd = index & 1
    order = lax.axis_index("head").astype(jnp.int32) ^ jnp.arange(n, dtype=jnp.int32)
    place = order ^ (odd * (n - 2))
    if n == blocks:
        halo = place
    else:
        halo = jnp.arange(blocks, dtype=jnp.int32) ^ (blocks - 2)
    has_far = jnp.logical_and(index > 0, index < lax.axis_size("blk") - 1)
    turn = jnp.stack([1 - 2 * odd, has_far.astype(jnp.int32)])

    kv = exchanged(packed(n, key_in, value))
    qd = exchanged(packed(n, query, grad_out))
    if n == blocks:
        groups = [stacked(kv[:-1]), kv[-1][None]]
        kv_far = [swapped(group, 1) for group in groups]
        kv_near = [swapped(group, 0) for group in groups]
        qd = stacked(qd, HINT)
        qd_far = swapped(qd, 1)
    else:
        local, qd = jnp.stack(kv), jnp.stack(qd)
        local = jnp.take(local, place, axis=0)
        kv_far = [swapped(local[:blocks], 1)]
        kv_near = [swapped(local[n - blocks:], 0)]
        qd_far = swapped(jnp.take(qd, place[:blocks], axis=0), 1)
    dq, stat, part, give = query_part(place, halo, turn, kv, qd, kv_far, kv_near)
    stat_far = swapped(stat[:, :, :HALF], 1)
    got = swapped(give, 0)
    dkv = key_part(place, halo, turn, kv, qd_far, stat_far, part, got)
    dq, dkv = lax.optimization_barrier((exchanged(dq), dkv))
    return *merged(dq), *merged(exchanged(dkv))


def solution(mesh):
    spec = P(("blk", "head"), None)
    return jax.shard_map(
        shards, mesh=mesh, in_specs=(spec,) * 4, out_specs=(spec,) * 3, check_vma=False
    )
```

```python
import math

import jax
import jax.numpy as jnp
from jax import lax
from jax.experimental import pallas as pl
from jax.experimental.pallas import tpu as pltpu
from jax.sharding import PartitionSpec as P

HEADS = 16
HEAD_DIM = 128
HALF = 512
TILE = 512
SUB = 256
SPAN = SUB + 2 * HALF
CHUNKS = SPAN // SUB
NEG = -1e30
HINT = 30_000_000_000
STRIP = 64
SCALE = HEAD_DIM ** -0.5
RATE = SCALE * math.log2(math.e)
VMEM_BYTES = 24 * 1024 * 1024
SMALL_BYTES = 8 * 1024 * 1024


def dot(a, b, contract):
    return lax.dot_general(
        a, b, ((contract[:1], contract[1:]), ((), ())), preferred_element_type=jnp.float32
    )


def rows_at(start, size):
    return pl.ds(pl.multiple_of(start, size), size)


def pack_kernel(*refs):
    ins, outs, sems = refs[:2], refs[2:-1], refs[-1]
    n = len(outs)
    width = outs[0].shape[2]
    me = lax.axis_index("head")
    copies = []
    for k, out in enumerate(outs):
        columns = pl.ds(pl.multiple_of((me ^ k) * width, 128), width)
        for which in range(2):
            copies.append(
                pltpu.make_async_copy(ins[which].at[:, columns], out.at[which], sems.at[2 * k + which])
            )
    for copy in copies:
        copy.start()
    for copy in copies:
        copy.wait()


def packed(n, first, second):
    r, width = first.shape[0], first.shape[1] // n
    return pl.pallas_call(
        pack_kernel,
        in_specs=[pl.BlockSpec(memory_space=pltpu.HBM)] * 2,
        out_specs=[pl.BlockSpec(memory_space=pltpu.VMEM)] * n,
        out_shape=[jax.ShapeDtypeStruct((2, r, width), first.dtype)] * n,
        scratch_shapes=[pltpu.SemaphoreType.DMA((2 * n,))],
        compiler_params=pltpu.CompilerParams(vmem_limit_bytes=SMALL_BYTES),
        name="pack",
    )(first, second)


def stack_kernel(*refs):
    n = (len(refs) - 2)
    ins, out, sems = refs[:n], refs[n], refs[n + 1]
    copies = [pltpu.make_async_copy(ins[k], out.at[k], sems.at[k]) for k in range(n)]
    for copy in copies:
        copy.start()
    for copy in copies:
        copy.wait()


def stacked(pieces, flops=0):
    n = len(pieces)
    return pl.pallas_call(
        stack_kernel,
        in_specs=[pl.BlockSpec(memory_space=pltpu.VMEM)] * n,
        out_specs=pl.BlockSpec(memory_space=pltpu.VMEM),
        out_shape=jax.ShapeDtypeStruct((n, *pieces[0].shape), pieces[0].dtype),
        scratch_shapes=[pltpu.SemaphoreType.DMA((n,))],
        compiler_params=pltpu.CompilerParams(vmem_limit_bytes=SMALL_BYTES),
        cost_estimate=pl.CostEstimate(flops=flops, bytes_accessed=0, transcendentals=0),
        name="stack",
    )(*pieces)


def merge_kernel(n, *refs):
    ins, outs, sems = refs[:n], refs[n:-1], refs[-1]
    width = ins[0].shape[-1]
    me = lax.axis_index("head")
    copies = []
    for k in range(n):
        columns = pl.ds(pl.multiple_of((me ^ k) * width, 128), width)
        for which, out in enumerate(outs):
            source = ins[k] if len(outs) == 1 else ins[k].at[which]
            copies.append(
                pltpu.make_async_copy(source, out.at[:, columns], sems.at[len(outs) * k + which])
            )
    for copy in copies:
        copy.start()
    for copy in copies:
        copy.wait()


def merged(pieces, flops=0):
    n = len(pieces)
    r, width = pieces[0].shape[-2:]
    count = 1 if pieces[0].ndim == 2 else 2
    return pl.pallas_call(
        lambda *refs: merge_kernel(n, *refs),
        in_specs=[pl.BlockSpec(memory_space=pltpu.VMEM)] * n,
        out_specs=[pl.BlockSpec(memory_space=pl.ANY)] * count,
        out_shape=[jax.ShapeDtypeStruct((r, n * width), pieces[0].dtype)] * count,
        scratch_shapes=[pltpu.SemaphoreType.DMA((count * n,))],
        compiler_params=pltpu.CompilerParams(vmem_limit_bytes=SMALL_BYTES),
        cost_estimate=pl.CostEstimate(flops=flops, bytes_accessed=0, transcendentals=0),
        name="merge",
    )(*pieces)


def ahead_by(turn_ref):
    return (
        lax.broadcasted_iota(jnp.int32, (SUB, SUB), 0)
        - lax.broadcasted_iota(jnp.int32, (SUB, SUB), 1)
    ) * turn_ref[0]


def members(refs):
    return [ref.at[i] for ref in refs for i in range(ref.shape[0])]


def query_kernel(n, groups, place_ref, halo_ref, turn_ref, *refs):
    kv_refs, refs = refs[:n], refs[n:]
    qd_ref, refs = refs[0], refs[1:]
    far_refs, near_refs, refs = refs[:groups], refs[groups:2 * groups], refs[2 * groups:]
    dq_refs, refs = refs[:n], refs[n:]
    stat_ref, part_ref, give_ref, k_ext, v_ext, k_flip, q_all, g_all, dq_all = refs[:9]
    s_buf, p_buf, w_buf, d_buf = refs[9:13]
    r, width = kv_refs[0].shape[1:]
    rows = n * r
    tiles = rows // TILE
    ahead = ahead_by(turn_ref)

    def each_head(h, _):
        lanes = rows_at(h * HEAD_DIM, HEAD_DIM)
        for i, (far, near) in enumerate(zip(members(far_refs), members(near_refs))):
            at = halo_ref[i] * r
            for which, ext in ((0, k_ext), (1, v_ext)):
                ext[rows_at(at, r)] = far[which, :, lanes]
                ext[rows_at(HALF + rows + at, r)] = near[which, :, lanes]
        for k in range(n):
            at = place_ref[k] * r
            for which, ext in ((0, k_ext), (1, v_ext)):
                ext[rows_at(HALF + at, r)] = kv_refs[k][which, :, lanes]
            q_all[rows_at(at, r)] = qd_ref[k, 0, :, lanes]
            g_all[rows_at(at, r)] = qd_ref[k, 1, :, lanes]
        k_flip[...] = k_ext[...].T
        if tiles > 1:
            refs[13][...] = jnp.zeros_like(refs[13])

        def each_tile(tile):
            first = tile * TILE
            has_far = turn_ref[1] > 0
            if tiles > 1:
                has_far = jnp.logical_or(has_far, tile > 0)

            def products(sub):
                here = rows_at(first + sub * SUB, SUB)
                query, grad = q_all[here], g_all[here]
                top = jnp.full((8, SUB), NEG, jnp.float32)
                for c in range(CHUNKS):
                    at = slice(c * SUB, (c + 1) * SUB)
                    keys = rows_at(first + (sub + c) * SUB, SUB)
                    s = dot(k_ext[keys], query, (1, 1)) * RATE
                    keep = None
                    if c == 0:
                        keep = ahead >= 0
                    if c == CHUNKS - 1:
                        keep = ahead <= 0
                    if sub + c < HALF // SUB:
                        keep = has_far if keep is None else jnp.logical_and(keep, has_far)
                    if keep is not None:
                        s = jnp.where(keep, s, NEG)
                    s_buf[sub, at] = s
                    top = jnp.maximum(top, jnp.max(s.reshape(SUB // 8, 8, SUB), axis=0))
                for c in range(CHUNKS):
                    at = slice(c * SUB, (c + 1) * SUB)
                    keys = rows_at(first + (sub + c) * SUB, SUB)
                    p_buf[sub, at] = dot(v_ext[keys], grad, (1, 1))
                return jnp.max(top, axis=0, keepdims=True)

            def softmax(sub, top):
                here = rows_at(first + sub * SUB, SUB)
                total = jnp.zeros((8, SUB), jnp.float32)
                delta = jnp.zeros((8, SUB), jnp.float32)
                for i in range(0, SPAN, STRIP):
                    at = slice(i, i + STRIP)
                    e = jnp.exp2(s_buf[sub, at] - top)
                    s_buf[sub, at] = e
                    total += jnp.sum(e.reshape(STRIP // 8, 8, SUB), axis=0)
                    delta += jnp.sum((e * p_buf[sub, at]).reshape(STRIP // 8, 8, SUB), axis=0)
                total = jnp.sum(total, axis=0, keepdims=True)
                inverse = 1.0 / total
                delta = jnp.sum(delta, axis=0, keepdims=True) * inverse
                stat_ref[h, 0:1, here] = top + jnp.log2(total)
                stat_ref[h, 1:2, here] = delta
                mine = slice(sub * SUB, (sub + 1) * SUB)
                for i in range(0, SPAN, STRIP):
                    at = slice(i, i + STRIP)
                    to = slice(sub * SUB + i, sub * SUB + i + STRIP)
                    w = s_buf[sub, at] * inverse
                    w_buf[to, mine] = w.astype(jnp.bfloat16)
                    d_buf[to, mine] = (w * (p_buf[sub, at] - delta)).astype(jnp.bfloat16)

            def query_grad(sub):
                mine = slice(sub * SUB, (sub + 1) * SUB)
                span = slice(sub * SUB, sub * SUB + SPAN)
                flip = k_flip[:, rows_at(first + sub * SUB, SPAN) if tiles > 1 else span]
                dq = dot(flip, d_buf[span, mine], (1, 0))
                here = rows_at(first + sub * SUB, SUB)
                dq_all[here] = (dq * SCALE).T.astype(jnp.bfloat16)

            tops = [products(sub) for sub in range(TILE // SUB)]
            for sub in range(TILE // SUB):
                softmax(sub, tops[sub])
                query_grad(sub)
            queries, grads = q_all[rows_at(first, TILE)], g_all[rows_at(first, TILE)]
            for which, buf, right in ((0, d_buf, queries), (1, w_buf, grads)):
                if tiles > 1:
                    acc = refs[13]
                    acc[which, rows_at(first, SUB)] += dot(buf[:SUB, :SUB], right[:SUB], (1, 0))
                    acc[which, rows_at(first + SUB, SPAN - SUB)] += dot(
                        buf[SUB:SPAN], right, (1, 0)
                    )
                    acc[which, rows_at(first + SPAN, SUB)] += dot(
                        buf[SPAN:, SUB:], right[SUB:], (1, 0)
                    )
                else:
                    part_ref[which, :, lanes] = dot(buf[HALF:HALF + TILE], right, (1, 0))
                    give_ref[which, :SUB, lanes] = dot(
                        buf[HALF + TILE:SPAN], right, (1, 0)
                    ).astype(jnp.bfloat16)
                    give_ref[which, SUB:, lanes] = dot(
                        buf[SPAN:, SUB:], right[SUB:], (1, 0)
                    ).astype(jnp.bfloat16)

        if tiles > 1:
            pl.loop(0, tiles)(each_tile)
            part_ref[:, :, lanes] = refs[13][:, HALF:HALF + rows]
            give_ref[:, :, lanes] = refs[13][:, HALF + rows:].astype(jnp.bfloat16)
        else:
            each_tile(0)
        for k in range(n):
            dq_refs[k][:, lanes] = dq_all[rows_at(place_ref[k] * r, r)]
        return 0

    lax.fori_loop(0, width // HEAD_DIM, each_head, 0)


def query_part(place, halo, turn, kv, qd, far, near):
    n = len(kv)
    _, r, width = kv[0].shape
    rows = n * r
    heads = width // HEAD_DIM
    ext = rows + 2 * HALF
    here, scalars = pl.BlockSpec(memory_space=pltpu.VMEM), pl.BlockSpec(memory_space=pltpu.SMEM)
    scratch = [
        pltpu.VMEM((ext, HEAD_DIM), jnp.bfloat16),
        pltpu.VMEM((ext, HEAD_DIM), jnp.bfloat16),
        pltpu.VMEM((HEAD_DIM, ext), jnp.bfloat16),
        pltpu.VMEM((rows, HEAD_DIM), jnp.bfloat16),
        pltpu.VMEM((rows, HEAD_DIM), jnp.bfloat16),
        pltpu.VMEM((rows, HEAD_DIM), jnp.bfloat16),
        pltpu.VMEM((TILE // SUB, SPAN, SUB), jnp.float32),
        pltpu.VMEM((TILE // SUB, SPAN, SUB), jnp.float32),
        pltpu.VMEM((TILE + 2 * HALF, TILE), jnp.bfloat16),
        pltpu.VMEM((TILE + 2 * HALF, TILE), jnp.bfloat16),
    ]
    if rows != TILE:
        scratch.append(pltpu.VMEM((2, ext, HEAD_DIM), jnp.float32))
    outs = pl.pallas_call(
        lambda *refs: query_kernel(n, len(far), *refs),
        in_specs=[scalars] * 3 + [here] * (n + 1 + 2 * len(far)),
        out_specs=[here] * (n + 3),
        scratch_shapes=scratch,
        out_shape=[jax.ShapeDtypeStruct((r, width), jnp.bfloat16)] * n
        + [
            jax.ShapeDtypeStruct((heads, 2, rows), jnp.float32),
            jax.ShapeDtypeStruct((2, rows, width), jnp.float32),
            jax.ShapeDtypeStruct((2, HALF, width), jnp.bfloat16),
        ],
        compiler_params=pltpu.CompilerParams(vmem_limit_bytes=VMEM_BYTES),
        cost_estimate=pl.CostEstimate(
            flops=10 * heads * rows * SPAN * HEAD_DIM,
            bytes_accessed=12 * rows * width,
            transcendentals=heads * rows * SPAN,
        ),
        name="query_part",
    )(place, halo, turn, *kv, qd, *far, *near)
    return outs[:n], outs[n], outs[n + 1], outs[n + 2]


def key_kernel(n, place_ref, halo_ref, turn_ref, *refs):
    kv_refs, refs = refs[:n], refs[n:]
    far_ref, stat_ref, part_ref, got_ref = refs[:4]
    out_refs, (k_all, v_all, q_all, g_all, acc, w_buf, d_buf) = refs[4:4 + n], refs[4 + n:]
    r, width = kv_refs[0].shape[1:]
    rows = n * r
    ahead = ahead_by(turn_ref)
    steps = HALF // SUB

    def each_head(h, _):
        lanes = rows_at(h * HEAD_DIM, HEAD_DIM)
        for k in range(n):
            at = rows_at(place_ref[k] * r, r)
            k_all[at] = kv_refs[k][0, :, lanes]
            v_all[at] = kv_refs[k][1, :, lanes]
        for i in range(HALF // r):
            at = rows_at(halo_ref[i] * r, r)
            q_all[at] = far_ref[i, 0, :, lanes]
            g_all[at] = far_ref[i, 1, :, lanes]
        acc[...] = part_ref[:, :, lanes]
        for a in range(steps):
            at = slice(rows - HALF + a * SUB, rows - HALF + (a + 1) * SUB)
            there = slice((steps - 1 - a) * SUB, (steps - a) * SUB)
            acc[:, at] += got_ref[:, there, lanes].astype(jnp.float32)
        for b in range(steps):
            here = slice(b * SUB, (b + 1) * SUB)
            there = slice((steps - 1 - b) * SUB, (steps - b) * SUB)
            query, grad = q_all[here], g_all[here]
            log_total = stat_ref[h, 0:1, there]
            delta = stat_ref[h, 1:2, there]
            for a in range(b + 1):
                at = slice(a * SUB, (a + 1) * SUB)
                w = jnp.exp2(dot(k_all[at], query, (1, 1)) * RATE - log_total)
                if a == b:
                    w = jnp.where(ahead <= 0, w, 0.0)
                w_buf[at, here] = w.astype(jnp.bfloat16)
                ds = w * (dot(v_all[at], grad, (1, 1)) - delta)
                d_buf[at, here] = ds.astype(jnp.bfloat16)
        for which, buf, right in ((0, d_buf, q_all), (1, w_buf, g_all)):
            for a in range(steps):
                at = slice(a * SUB, (a + 1) * SUB)
                acc[which, at] += dot(buf[at, a * SUB:], right[a * SUB:], (1, 0))
        for k in range(n):
            at = rows_at(place_ref[k] * r, r)
            out_refs[k][0, :, lanes] = (acc[0, at] * SCALE).astype(jnp.bfloat16)
            out_refs[k][1, :, lanes] = acc[1, at].astype(jnp.bfloat16)
        return 0

    lax.fori_loop(0, width // HEAD_DIM, each_head, 0)


def key_part(place, halo, turn, kv, far, stat, part, got):
    n = len(kv)
    _, r, width = kv[0].shape
    rows = n * r
    heads = width // HEAD_DIM
    here, scalars = pl.BlockSpec(memory_space=pltpu.VMEM), pl.BlockSpec(memory_space=pltpu.SMEM)
    return pl.pallas_call(
        lambda *refs: key_kernel(n, *refs),
        in_specs=[scalars] * 3 + [here] * (n + 4),
        out_specs=[here] * n,
        scratch_shapes=[
            pltpu.VMEM((rows, HEAD_DIM), jnp.bfloat16),
            pltpu.VMEM((rows, HEAD_DIM), jnp.bfloat16),
            pltpu.VMEM((HALF, HEAD_DIM), jnp.bfloat16),
            pltpu.VMEM((HALF, HEAD_DIM), jnp.bfloat16),
            pltpu.VMEM((2, rows, HEAD_DIM), jnp.float32),
            pltpu.VMEM((HALF, HALF), jnp.bfloat16),
            pltpu.VMEM((HALF, HALF), jnp.bfloat16),
        ],
        out_shape=[jax.ShapeDtypeStruct((2, r, width), jnp.bfloat16)] * n,
        compiler_params=pltpu.CompilerParams(vmem_limit_bytes=VMEM_BYTES),
        cost_estimate=pl.CostEstimate(
            flops=HINT,
            bytes_accessed=24 * rows * width,
            transcendentals=heads * HALF * (HALF // 2 + SUB // 2),
        ),
        name="key_part",
    )(place, halo, turn, *kv, far, stat, part, got)


def swapped(array, first):
    count = lax.axis_size("blk")
    pairs = [(i, i + 1) for i in range(first, count - 1, 2)]
    return lax.ppermute(array, "blk", pairs + [(j, i) for i, j in pairs])


def exchanged(pieces):
    n = len(pieces)
    moved = {
        k: lax.ppermute(pieces[k], "head", [(i, i ^ k) for i in range(n)])
        for k in range(1, n)
    }
    return [pieces[0]] + [moved[k] for k in range(1, n)]


def shards(query, key_in, value, grad_out):
    n = lax.axis_size("head")
    blocks = HALF // query.shape[0]
    index = lax.axis_index("blk").astype(jnp.int32)
    odd = index & 1
    order = lax.axis_index("head").astype(jnp.int32) ^ jnp.arange(n, dtype=jnp.int32)
    place = order ^ (odd * (n - 2))
    if n == blocks:
        halo = place
    else:
        halo = jnp.arange(blocks, dtype=jnp.int32) ^ (blocks - 2)
    has_far = jnp.logical_and(index > 0, index < lax.axis_size("blk") - 1)
    turn = jnp.stack([1 - 2 * odd, has_far.astype(jnp.int32)])

    kv = exchanged(packed(n, key_in, value))
    qd = exchanged(packed(n, query, grad_out))
    if n == blocks:
        groups = [stacked(kv[:-1]), kv[-1][None]]
        kv_far = [swapped(group, 1) for group in groups]
        kv_near = [swapped(group, 0) for group in groups]
        qd = stacked(qd, HINT)
        qd_far = swapped(qd, 1)
        key_halo = place
    else:
        local, qd = jnp.stack(kv), jnp.stack(qd)
        local = jnp.take(local, place, axis=0)
        kv_far = [swapped(local[:blocks], 1)]
        kv_near = [swapped(local[n - blocks:], 0)]
        qd_far = swapped(jnp.take(qd, place[:blocks], axis=0), 1)
        key_halo = halo
    dq, stat, part, give = query_part(place, halo, turn, kv, qd, kv_far, kv_near)
    stat_far = swapped(stat[:, :, :HALF], 1)
    got = swapped(give, 0)
    dkv = key_part(place, key_halo, turn, kv, qd_far, stat_far, part, got)
    return *merged(exchanged(dq), HINT), *merged(exchanged(dkv))


def solution(mesh):
    spec = P(("blk", "head"), None)
    return jax.shard_map(
        shards, mesh=mesh, in_specs=(spec,) * 4, out_specs=(spec,) * 3, check_vma=False
    )
```

```python
import math

import jax
import jax.numpy as jnp
from jax import lax
from jax.experimental import pallas as pl
from jax.experimental.pallas import tpu as pltpu
from jax.sharding import PartitionSpec as P

HEADS = 16
HEAD_DIM = 128
HALF = 512
TILE = 512
SUB = 256
SPAN = SUB + 2 * HALF
CHUNKS = SPAN // SUB
NEG = -1e30
HINT = 30_000_000_000
STRIP = 64
UNIT = 128
UNITS = SPAN // UNIT
SCALE = HEAD_DIM ** -0.5
RATE = SCALE * math.log2(math.e)
VMEM_BYTES = 24 * 1024 * 1024
SMALL_BYTES = 8 * 1024 * 1024


def dot(a, b, contract):
    return lax.dot_general(
        a, b, ((contract[:1], contract[1:]), ((), ())), preferred_element_type=jnp.float32
    )


def rows_at(start, size):
    return pl.ds(pl.multiple_of(start, size), size)


def pack_kernel(*refs):
    ins, outs, sems = refs[:2], refs[2:-1], refs[-1]
    n = len(outs)
    width = outs[0].shape[2]
    me = lax.axis_index("head")
    copies = []
    for k, out in enumerate(outs):
        columns = pl.ds(pl.multiple_of((me ^ k) * width, 128), width)
        for which in range(2):
            copies.append(
                pltpu.make_async_copy(ins[which].at[:, columns], out.at[which], sems.at[2 * k + which])
            )
    for copy in copies:
        copy.start()
    for copy in copies:
        copy.wait()


def packed(n, first, second):
    r, width = first.shape[0], first.shape[1] // n
    return pl.pallas_call(
        pack_kernel,
        in_specs=[pl.BlockSpec(memory_space=pltpu.HBM)] * 2,
        out_specs=[pl.BlockSpec(memory_space=pltpu.VMEM)] * n,
        out_shape=[jax.ShapeDtypeStruct((2, r, width), first.dtype)] * n,
        scratch_shapes=[pltpu.SemaphoreType.DMA((2 * n,))],
        compiler_params=pltpu.CompilerParams(vmem_limit_bytes=SMALL_BYTES),
        name="pack",
    )(first, second)


def stack_kernel(*refs):
    n = (len(refs) - 2)
    ins, out, sems = refs[:n], refs[n], refs[n + 1]
    copies = [pltpu.make_async_copy(ins[k], out.at[k], sems.at[k]) for k in range(n)]
    for copy in copies:
        copy.start()
    for copy in copies:
        copy.wait()


def stacked(pieces, flops=0):
    n = len(pieces)
    return pl.pallas_call(
        stack_kernel,
        in_specs=[pl.BlockSpec(memory_space=pltpu.VMEM)] * n,
        out_specs=pl.BlockSpec(memory_space=pltpu.VMEM),
        out_shape=jax.ShapeDtypeStruct((n, *pieces[0].shape), pieces[0].dtype),
        scratch_shapes=[pltpu.SemaphoreType.DMA((n,))],
        compiler_params=pltpu.CompilerParams(vmem_limit_bytes=SMALL_BYTES),
        cost_estimate=pl.CostEstimate(flops=flops, bytes_accessed=0, transcendentals=0),
        name="stack",
    )(*pieces)


def merge_kernel(n, *refs):
    ins, outs, sems = refs[:n], refs[n:-1], refs[-1]
    width = ins[0].shape[-1]
    me = lax.axis_index("head")
    copies = []
    for k in range(n):
        columns = pl.ds(pl.multiple_of((me ^ k) * width, 128), width)
        for which, out in enumerate(outs):
            source = ins[k] if len(outs) == 1 else ins[k].at[which]
            copies.append(
                pltpu.make_async_copy(source, out.at[:, columns], sems.at[len(outs) * k + which])
            )
    for copy in copies:
        copy.start()
    for copy in copies:
        copy.wait()


def merged(pieces, flops=0):
    n = len(pieces)
    r, width = pieces[0].shape[-2:]
    count = 1 if pieces[0].ndim == 2 else 2
    return pl.pallas_call(
        lambda *refs: merge_kernel(n, *refs),
        in_specs=[pl.BlockSpec(memory_space=pltpu.VMEM)] * n,
        out_specs=[pl.BlockSpec(memory_space=pl.ANY)] * count,
        out_shape=[jax.ShapeDtypeStruct((r, n * width), pieces[0].dtype)] * count,
        scratch_shapes=[pltpu.SemaphoreType.DMA((count * n,))],
        compiler_params=pltpu.CompilerParams(vmem_limit_bytes=SMALL_BYTES),
        cost_estimate=pl.CostEstimate(flops=flops, bytes_accessed=0, transcendentals=0),
        name="merge",
    )(*pieces)


def ahead_by(turn_ref):
    return (
        lax.broadcasted_iota(jnp.int32, (SUB, SUB), 0)
        - lax.broadcasted_iota(jnp.int32, (SUB, SUB), 1)
    ) * turn_ref[0]


def members(refs):
    return [ref.at[i] for ref in refs for i in range(ref.shape[0])]


def query_kernel(n, groups, place_ref, halo_ref, turn_ref, *refs):
    kv_refs, refs = refs[:n], refs[n:]
    qd_ref, refs = refs[0], refs[1:]
    far_refs, near_refs, refs = refs[:groups], refs[groups:2 * groups], refs[2 * groups:]
    dq_refs, refs = refs[:n], refs[n:]
    stat_ref, part_ref, give_ref, k_ext, v_ext, k_flip, q_all, g_all, dq_all = refs[:9]
    s_buf, p_buf, w_buf, d_buf, n_buf = refs[9:14]
    r, width = kv_refs[0].shape[1:]
    rows = n * r
    tiles = rows // TILE
    ahead = ahead_by(turn_ref)

    def each_head(h, _):
        lanes = rows_at(h * HEAD_DIM, HEAD_DIM)
        for i, (far, near) in enumerate(zip(members(far_refs), members(near_refs))):
            at = halo_ref[i] * r
            for which, ext in ((0, k_ext), (1, v_ext)):
                ext[rows_at(at, r)] = far[which, :, lanes]
                ext[rows_at(HALF + rows + at, r)] = near[which, :, lanes]
        for k in range(n):
            at = place_ref[k] * r
            for which, ext in ((0, k_ext), (1, v_ext)):
                ext[rows_at(HALF + at, r)] = kv_refs[k][which, :, lanes]
            q_all[rows_at(at, r)] = qd_ref[k, 0, :, lanes]
            g_all[rows_at(at, r)] = qd_ref[k, 1, :, lanes]
        k_flip[...] = k_ext[...].T
        if tiles > 1:
            refs[14][...] = jnp.zeros_like(refs[14])

        def each_tile(tile):
            first = tile * TILE
            has_far = turn_ref[1] > 0
            if tiles > 1:
                has_far = jnp.logical_or(has_far, tile > 0)

            subs = range(TILE // SUB)
            heres = [rows_at(first + sub * SUB, SUB) for sub in subs]
            query = [q_all[here] for here in heres]
            grad = [g_all[here] for here in heres]
            tops = [[] for _ in subs]
            totals = [[] for _ in subs]
            deltas = [[] for _ in subs]
            ready = {}

            def folded(x, op):
                return op(x.reshape(x.shape[0] // 8, 8, SUB), axis=0)

            def score(sub, u):
                keys = rows_at(first + sub * SUB + u * UNIT, UNIT)
                s = dot(k_ext[keys], query[sub], (1, 1)) * RATE
                keep = None
                c = u * UNIT // SUB
                inside = slice(u * UNIT % SUB, u * UNIT % SUB + UNIT)
                if c == 0:
                    keep = ahead[inside] >= 0
                if c == CHUNKS - 1:
                    keep = ahead[inside] <= 0
                if sub + c < HALF // SUB:
                    keep = has_far if keep is None else jnp.logical_and(keep, has_far)
                if keep is not None:
                    s = jnp.where(keep, s, NEG)
                top = jnp.max(folded(s, jnp.max), axis=0, keepdims=True)
                e = jnp.exp2(s - top)
                s_buf[sub, u * UNIT:(u + 1) * UNIT] = e
                tops[sub].append(top)
                totals[sub].append(folded(e, jnp.sum))

            def product(sub, u):
                keys = rows_at(first + sub * SUB + u * UNIT, UNIT)
                at = slice(u * UNIT, (u + 1) * UNIT)
                dp = dot(v_ext[keys], grad[sub], (1, 1))
                p_buf[sub, at] = dp
                deltas[sub].append(folded(s_buf[sub, at] * dp, jnp.sum))

            def settle(sub):
                top = tops[sub][0]
                for other in tops[sub][1:]:
                    top = jnp.maximum(top, other)
                parts = [jnp.exp2(other - top) for other in tops[sub]]
                total = sum(p * t for p, t in zip(parts, totals[sub]))
                total = jnp.sum(total, axis=0, keepdims=True)
                inverse = 1.0 / total
                delta = sum(p * d for p, d in zip(parts, deltas[sub]))
                delta = jnp.sum(delta, axis=0, keepdims=True) * inverse
                stat_ref[h, 0:1, heres[sub]] = top + jnp.log2(total)
                stat_ref[h, 1:2, heres[sub]] = delta
                ready[sub] = [p * inverse for p in parts], delta

            def weigh(sub, u):
                mine = slice(sub * SUB, (sub + 1) * SUB)
                parts, delta = ready[sub]
                for i in range(u * UNIT, (u + 1) * UNIT, STRIP):
                    at = slice(i, i + STRIP)
                    to = slice(sub * SUB + i, sub * SUB + i + STRIP)
                    w = s_buf[sub, at] * parts[u]
                    w_buf[to, mine] = w.astype(jnp.bfloat16)
                    d_buf[to, mine] = (w * (p_buf[sub, at] - delta)).astype(jnp.bfloat16)

            def query_grad(sub):
                mine = slice(sub * SUB, (sub + 1) * SUB)
                span = slice(sub * SUB, sub * SUB + SPAN)
                flip = k_flip[:, rows_at(first + sub * SUB, SPAN) if tiles > 1 else span]
                dq = dot(flip, d_buf[span, mine], (1, 0))
                dq_all[heres[sub]] = (dq * SCALE).T.astype(jnp.bfloat16)

            def key_grads(sub):
                mine = slice(sub * SUB, (sub + 1) * SUB)
                for which, buf, right in ((0, d_buf, query[sub]), (1, w_buf, grad[sub])):
                    if tiles > 1:
                        spot = rows_at(first + sub * SUB, SPAN)
                        refs[14][which, spot] += dot(
                            buf[sub * SUB:sub * SUB + SPAN, mine], right, (1, 0)
                        )
                        continue
                    own = dot(buf[HALF:HALF + TILE, mine], right, (1, 0))
                    near = dot(buf[HALF + TILE:SPAN + sub * SUB, mine], right, (1, 0))
                    if sub == 0:
                        part_ref[which, :, lanes] = own
                        n_buf[which] = near
                    else:
                        part_ref[which, :, lanes] += own
                        near0 = n_buf[which] + near[:SUB]
                        give_ref[which, :SUB, lanes] = near0.astype(jnp.bfloat16)
                        give_ref[which, SUB:, lanes] = near[SUB:].astype(jnp.bfloat16)

            every = range(UNITS)
            for sub in subs:
                for u in every:
                    score(sub, u)
                    product(sub, u)
            for sub in subs:
                settle(sub)
                for u in every:
                    weigh(sub, u)
            for sub in subs:
                query_grad(sub)
                key_grads(sub)

        if tiles > 1:
            pl.loop(0, tiles)(each_tile)
            part_ref[:, :, lanes] = refs[14][:, HALF:HALF + rows]
            give_ref[:, :, lanes] = refs[14][:, HALF + rows:].astype(jnp.bfloat16)
        else:
            each_tile(0)
        for k in range(n):
            dq_refs[k][:, lanes] = dq_all[rows_at(place_ref[k] * r, r)]
        return 0

    lax.fori_loop(0, width // HEAD_DIM, each_head, 0)


def query_part(place, halo, turn, kv, qd, far, near):
    n = len(kv)
    _, r, width = kv[0].shape
    rows = n * r
    heads = width // HEAD_DIM
    ext = rows + 2 * HALF
    here, scalars = pl.BlockSpec(memory_space=pltpu.VMEM), pl.BlockSpec(memory_space=pltpu.SMEM)
    scratch = [
        pltpu.VMEM((ext, HEAD_DIM), jnp.bfloat16),
        pltpu.VMEM((ext, HEAD_DIM), jnp.bfloat16),
        pltpu.VMEM((HEAD_DIM, ext), jnp.bfloat16),
        pltpu.VMEM((rows, HEAD_DIM), jnp.bfloat16),
        pltpu.VMEM((rows, HEAD_DIM), jnp.bfloat16),
        pltpu.VMEM((rows, HEAD_DIM), jnp.bfloat16),
        pltpu.VMEM((TILE // SUB, SPAN, SUB), jnp.float32),
        pltpu.VMEM((TILE // SUB, SPAN, SUB), jnp.float32),
        pltpu.VMEM((TILE + 2 * HALF, TILE), jnp.bfloat16),
        pltpu.VMEM((TILE + 2 * HALF, TILE), jnp.bfloat16),
        pltpu.VMEM((2, SUB, HEAD_DIM), jnp.float32),
    ]
    if rows != TILE:
        scratch.append(pltpu.VMEM((2, ext, HEAD_DIM), jnp.float32))
    outs = pl.pallas_call(
        lambda *refs: query_kernel(n, len(far), *refs),
        in_specs=[scalars] * 3 + [here] * (n + 1 + 2 * len(far)),
        out_specs=[here] * (n + 3),
        scratch_shapes=scratch,
        out_shape=[jax.ShapeDtypeStruct((r, width), jnp.bfloat16)] * n
        + [
            jax.ShapeDtypeStruct((heads, 2, rows), jnp.float32),
            jax.ShapeDtypeStruct((2, rows, width), jnp.float32),
            jax.ShapeDtypeStruct((2, HALF, width), jnp.bfloat16),
        ],
        compiler_params=pltpu.CompilerParams(vmem_limit_bytes=VMEM_BYTES),
        cost_estimate=pl.CostEstimate(
            flops=10 * heads * rows * SPAN * HEAD_DIM,
            bytes_accessed=12 * rows * width,
            transcendentals=heads * rows * SPAN,
        ),
        name="query_part",
    )(place, halo, turn, *kv, qd, *far, *near)
    return outs[:n], outs[n], outs[n + 1], outs[n + 2]


def key_kernel(n, place_ref, halo_ref, turn_ref, *refs):
    kv_refs, refs = refs[:n], refs[n:]
    far_ref, stat_ref, part_ref, got_ref = refs[:4]
    out_refs, (k_all, v_all, q_all, g_all, acc, w_buf, d_buf) = refs[4:4 + n], refs[4 + n:]
    r, width = kv_refs[0].shape[1:]
    rows = n * r
    ahead = ahead_by(turn_ref)
    steps = HALF // SUB

    def each_head(h, _):
        lanes = rows_at(h * HEAD_DIM, HEAD_DIM)
        for k in range(n):
            at = rows_at(place_ref[k] * r, r)
            k_all[at] = kv_refs[k][0, :, lanes]
            v_all[at] = kv_refs[k][1, :, lanes]
        for i in range(HALF // r):
            at = rows_at(halo_ref[i] * r, r)
            q_all[at] = far_ref[i, 0, :, lanes]
            g_all[at] = far_ref[i, 1, :, lanes]
        acc[...] = part_ref[:, :, lanes]
        for a in range(steps):
            at = slice(rows - HALF + a * SUB, rows - HALF + (a + 1) * SUB)
            there = slice((steps - 1 - a) * SUB, (steps - a) * SUB)
            acc[:, at] += got_ref[:, there, lanes].astype(jnp.float32)
        for b in range(steps):
            here = slice(b * SUB, (b + 1) * SUB)
            there = slice((steps - 1 - b) * SUB, (steps - b) * SUB)
            query, grad = q_all[here], g_all[here]
            log_total = jnp.where(turn_ref[1] > 0, stat_ref[h, 0:1, there], -NEG)
            delta = stat_ref[h, 1:2, there]
            for a in range(b + 1):
                at = slice(a * SUB, (a + 1) * SUB)
                w = jnp.exp2(dot(k_all[at], query, (1, 1)) * RATE - log_total)
                if a == b:
                    w = jnp.where(ahead <= 0, w, 0.0)
                w_buf[at, here] = w.astype(jnp.bfloat16)
                ds = w * (dot(v_all[at], grad, (1, 1)) - delta)
                d_buf[at, here] = ds.astype(jnp.bfloat16)
        for which, buf, right in ((0, d_buf, q_all), (1, w_buf, g_all)):
            for a in range(steps):
                at = slice(a * SUB, (a + 1) * SUB)
                acc[which, at] += dot(buf[at, a * SUB:], right[a * SUB:], (1, 0))
        for k in range(n):
            at = rows_at(place_ref[k] * r, r)
            out_refs[k][0, :, lanes] = (acc[0, at] * SCALE).astype(jnp.bfloat16)
            out_refs[k][1, :, lanes] = acc[1, at].astype(jnp.bfloat16)
        return 0

    lax.fori_loop(0, width // HEAD_DIM, each_head, 0)


def key_part(place, halo, turn, kv, far, stat, part, got):
    n = len(kv)
    _, r, width = kv[0].shape
    rows = n * r
    heads = width // HEAD_DIM
    here, scalars = pl.BlockSpec(memory_space=pltpu.VMEM), pl.BlockSpec(memory_space=pltpu.SMEM)
    return pl.pallas_call(
        lambda *refs: key_kernel(n, *refs),
        in_specs=[scalars] * 3 + [here] * (n + 4),
        out_specs=[here] * n,
        scratch_shapes=[
            pltpu.VMEM((rows, HEAD_DIM), jnp.bfloat16),
            pltpu.VMEM((rows, HEAD_DIM), jnp.bfloat16),
            pltpu.VMEM((HALF, HEAD_DIM), jnp.bfloat16),
            pltpu.VMEM((HALF, HEAD_DIM), jnp.bfloat16),
            pltpu.VMEM((2, rows, HEAD_DIM), jnp.float32),
            pltpu.VMEM((HALF, HALF), jnp.bfloat16),
            pltpu.VMEM((HALF, HALF), jnp.bfloat16),
        ],
        out_shape=[jax.ShapeDtypeStruct((2, r, width), jnp.bfloat16)] * n,
        compiler_params=pltpu.CompilerParams(vmem_limit_bytes=VMEM_BYTES),
        cost_estimate=pl.CostEstimate(
            flops=HINT,
            bytes_accessed=24 * rows * width,
            transcendentals=heads * HALF * (HALF // 2 + SUB // 2),
        ),
        name="key_part",
    )(place, halo, turn, *kv, far, stat, part, got)


def swapped(array, first, idle=False):
    count, n = lax.axis_size("blk"), lax.axis_size("head")
    pairs = []
    for h in range(n):
        for b in range(count):
            other = b + 1 if b % 2 == first else b - 1
            if 0 <= other < count:
                pairs.append((h * count + b, h * count + other))
            elif idle:
                pairs.append((h * count + b, (h ^ 1) * count + b))
    return lax.ppermute(array, ("head", "blk"), pairs)


def exchanged(pieces):
    n = len(pieces)
    moved = {
        k: lax.ppermute(pieces[k], "head", [(i, i ^ k) for i in range(n)])
        for k in range(1, n)
    }
    return [pieces[0]] + [moved[k] for k in range(1, n)]


def shards(query, key_in, value, grad_out):
    n = lax.axis_size("head")
    blocks = HALF // query.shape[0]
    index = lax.axis_index("blk").astype(jnp.int32)
    odd = index & 1
    order = lax.axis_index("head").astype(jnp.int32) ^ jnp.arange(n, dtype=jnp.int32)
    place = order ^ (odd * (n - 2))
    if n == blocks:
        halo = place
    else:
        halo = jnp.arange(blocks, dtype=jnp.int32) ^ (blocks - 2)
    has_far = jnp.logical_and(index > 0, index < lax.axis_size("blk") - 1)
    turn = jnp.stack([1 - 2 * odd, has_far.astype(jnp.int32)])

    kv = exchanged(packed(n, key_in, value))
    qd = exchanged(packed(n, query, grad_out))
    if n == blocks:
        groups = [stacked(kv[:-1]), kv[-1][None]]
        kv_far = [swapped(groups[0], 1), swapped(groups[1], 1, True)]
        kv_near = [swapped(group, 0) for group in groups]
        qd = stacked(qd, HINT)
        qd_far = swapped(qd, 1, True)
        key_halo = place
    else:
        local, qd = jnp.stack(kv), jnp.stack(qd)
        local = jnp.take(local, place, axis=0)
        kv_far = [swapped(local[:blocks], 1)]
        kv_near = [swapped(local[n - blocks:], 0)]
        qd_far = swapped(jnp.take(qd, place[:blocks], axis=0), 1, True)
        key_halo = halo
    dq, stat, part, give = query_part(place, halo, turn, kv, qd, kv_far, kv_near)
    stat_far = swapped(stat[:, :, :HALF], 1, True)
    got = swapped(give, 0)
    dkv = key_part(place, key_halo, turn, kv, qd_far, stat_far, part, got)
    return *merged(exchanged(dq), HINT), *merged(exchanged(dkv))


def solution(mesh):
    spec = P(("blk", "head"), None)
    return jax.shard_map(
        shards, mesh=mesh, in_specs=(spec,) * 4, out_specs=(spec,) * 3, check_vma=False
    )
```

```python
import math

import jax
import jax.numpy as jnp
from jax import lax
from jax.experimental import pallas as pl
from jax.experimental.pallas import tpu as pltpu
from jax.sharding import PartitionSpec as P

HEADS = 16
HEAD_DIM = 128
HALF = 512
TILE = 512
SUB = 256
SPAN = SUB + 2 * HALF
CHUNKS = SPAN // SUB
NEG = -1e30
HINT = 30_000_000_000
STRIP = 64
UNIT = 128
UNITS = SPAN // UNIT
SCALE = HEAD_DIM ** -0.5
RATE = SCALE * math.log2(math.e)
VMEM_BYTES = 46 * 1024 * 1024
QGROUP = 4
KGROUP = 4
SMALL_BYTES = 8 * 1024 * 1024


def dot(a, b, contract):
    return lax.dot_general(
        a, b, ((contract[:1], contract[1:]), ((), ())), preferred_element_type=jnp.float32
    )


def rows_at(start, size):
    return pl.ds(pl.multiple_of(start, size), size)


def pack_kernel(*refs):
    ins, outs, sems = refs[:2], refs[2:-1], refs[-1]
    n = len(outs)
    width = outs[0].shape[2]
    me = lax.axis_index("head")
    copies = []
    for k, out in enumerate(outs):
        columns = pl.ds(pl.multiple_of((me ^ k) * width, 128), width)
        for which in range(2):
            copies.append(
                pltpu.make_async_copy(ins[which].at[:, columns], out.at[which], sems.at[2 * k + which])
            )
    for copy in copies:
        copy.start()
    for copy in copies:
        copy.wait()


def packed(n, first, second):
    r, width = first.shape[0], first.shape[1] // n
    return pl.pallas_call(
        pack_kernel,
        in_specs=[pl.BlockSpec(memory_space=pltpu.HBM)] * 2,
        out_specs=[pl.BlockSpec(memory_space=pltpu.VMEM)] * n,
        out_shape=[jax.ShapeDtypeStruct((2, r, width), first.dtype)] * n,
        scratch_shapes=[pltpu.SemaphoreType.DMA((2 * n,))],
        compiler_params=pltpu.CompilerParams(vmem_limit_bytes=SMALL_BYTES),
        name="pack",
    )(first, second)


def stack_kernel(*refs):
    n = (len(refs) - 2)
    ins, out, sems = refs[:n], refs[n], refs[n + 1]
    copies = [pltpu.make_async_copy(ins[k], out.at[k], sems.at[k]) for k in range(n)]
    for copy in copies:
        copy.start()
    for copy in copies:
        copy.wait()


def stacked(pieces, flops=0):
    n = len(pieces)
    return pl.pallas_call(
        stack_kernel,
        in_specs=[pl.BlockSpec(memory_space=pltpu.VMEM)] * n,
        out_specs=pl.BlockSpec(memory_space=pltpu.VMEM),
        out_shape=jax.ShapeDtypeStruct((n, *pieces[0].shape), pieces[0].dtype),
        scratch_shapes=[pltpu.SemaphoreType.DMA((n,))],
        compiler_params=pltpu.CompilerParams(vmem_limit_bytes=SMALL_BYTES),
        cost_estimate=pl.CostEstimate(flops=flops, bytes_accessed=0, transcendentals=0),
        name="stack",
    )(*pieces)


def merge_kernel(n, *refs):
    ins, outs, sems = refs[:n], refs[n:-1], refs[-1]
    width = ins[0].shape[-1]
    me = lax.axis_index("head")
    copies = []
    for k in range(n):
        columns = pl.ds(pl.multiple_of((me ^ k) * width, 128), width)
        for which, out in enumerate(outs):
            source = ins[k] if len(outs) == 1 else ins[k].at[which]
            copies.append(
                pltpu.make_async_copy(source, out.at[:, columns], sems.at[len(outs) * k + which])
            )
    for copy in copies:
        copy.start()
    for copy in copies:
        copy.wait()


def merged(pieces, flops=0):
    n = len(pieces)
    r, width = pieces[0].shape[-2:]
    count = 1 if pieces[0].ndim == 2 else 2
    return pl.pallas_call(
        lambda *refs: merge_kernel(n, *refs),
        in_specs=[pl.BlockSpec(memory_space=pltpu.VMEM)] * n,
        out_specs=[pl.BlockSpec(memory_space=pl.ANY)] * count,
        out_shape=[jax.ShapeDtypeStruct((r, n * width), pieces[0].dtype)] * count,
        scratch_shapes=[pltpu.SemaphoreType.DMA((count * n,))],
        compiler_params=pltpu.CompilerParams(vmem_limit_bytes=SMALL_BYTES),
        cost_estimate=pl.CostEstimate(flops=flops, bytes_accessed=0, transcendentals=0),
        name="merge",
    )(*pieces)


def ahead_by(turn_ref):
    return (
        lax.broadcasted_iota(jnp.int32, (SUB, SUB), 0)
        - lax.broadcasted_iota(jnp.int32, (SUB, SUB), 1)
    ) * turn_ref[0]


def over_heads(heads, scratch, each_head):
    group = scratch[0].shape[0]

    def each_group(i, _):
        for member in range(group):
            each_head(i * group + member, [ref.at[member] for ref in scratch])
        return 0

    lax.fori_loop(0, heads // group, each_group, 0)


def members(refs):
    return [ref.at[i] for ref in refs for i in range(ref.shape[0])]


def query_kernel(n, groups, place_ref, halo_ref, turn_ref, *refs):
    kv_refs, refs = refs[:n], refs[n:]
    qd_ref, refs = refs[0], refs[1:]
    far_refs, near_refs, refs = refs[:groups], refs[groups:2 * groups], refs[2 * groups:]
    dq_refs, refs = refs[:n], refs[n:]
    stat_ref, part_ref, give_ref = refs[:3]
    r, width = kv_refs[0].shape[1:]
    rows = n * r
    tiles = rows // TILE
    ahead = ahead_by(turn_ref)

    def each_head(h, scratch):
        k_ext, v_ext, k_flip, q_all, g_all, dq_all = scratch[:6]
        s_buf, p_buf, w_buf, d_buf, n_buf = scratch[6:11]
        lanes = rows_at(h * HEAD_DIM, HEAD_DIM)
        for i, (far, near) in enumerate(zip(members(far_refs), members(near_refs))):
            at = halo_ref[i] * r
            for which, ext in ((0, k_ext), (1, v_ext)):
                ext[rows_at(at, r)] = far[which, :, lanes]
                ext[rows_at(HALF + rows + at, r)] = near[which, :, lanes]
        for k in range(n):
            at = place_ref[k] * r
            for which, ext in ((0, k_ext), (1, v_ext)):
                ext[rows_at(HALF + at, r)] = kv_refs[k][which, :, lanes]
            q_all[rows_at(at, r)] = qd_ref[k, 0, :, lanes]
            g_all[rows_at(at, r)] = qd_ref[k, 1, :, lanes]
        k_flip[...] = k_ext[...].T
        if tiles > 1:
            scratch[11][...] = jnp.zeros_like(scratch[11])

        def each_tile(tile):
            first = tile * TILE
            has_far = turn_ref[1] > 0
            if tiles > 1:
                has_far = jnp.logical_or(has_far, tile > 0)

            subs = range(TILE // SUB)
            heres = [rows_at(first + sub * SUB, SUB) for sub in subs]
            query = [q_all[here] for here in heres]
            grad = [g_all[here] for here in heres]
            tops = [[] for _ in subs]
            totals = [[] for _ in subs]
            deltas = [[] for _ in subs]
            ready = {}

            def folded(x, op):
                return op(x.reshape(x.shape[0] // 8, 8, SUB), axis=0)

            def score(sub, u):
                keys = rows_at(first + sub * SUB + u * UNIT, UNIT)
                s = dot(k_ext[keys], query[sub], (1, 1)) * RATE
                keep = None
                c = u * UNIT // SUB
                inside = slice(u * UNIT % SUB, u * UNIT % SUB + UNIT)
                if c == 0:
                    keep = ahead[inside] >= 0
                if c == CHUNKS - 1:
                    keep = ahead[inside] <= 0
                if sub + c < HALF // SUB:
                    keep = has_far if keep is None else jnp.logical_and(keep, has_far)
                if keep is not None:
                    s = jnp.where(keep, s, NEG)
                top = jnp.max(folded(s, jnp.max), axis=0, keepdims=True)
                e = jnp.exp2(s - top)
                s_buf[sub, u * UNIT:(u + 1) * UNIT] = e
                tops[sub].append(top)
                totals[sub].append(folded(e, jnp.sum))

            def product(sub, u):
                keys = rows_at(first + sub * SUB + u * UNIT, UNIT)
                at = slice(u * UNIT, (u + 1) * UNIT)
                dp = dot(v_ext[keys], grad[sub], (1, 1))
                p_buf[sub, at] = dp
                deltas[sub].append(folded(s_buf[sub, at] * dp, jnp.sum))

            def settle(sub):
                top = tops[sub][0]
                for other in tops[sub][1:]:
                    top = jnp.maximum(top, other)
                parts = [jnp.exp2(other - top) for other in tops[sub]]
                total = sum(p * t for p, t in zip(parts, totals[sub]))
                total = jnp.sum(total, axis=0, keepdims=True)
                inverse = 1.0 / total
                delta = sum(p * d for p, d in zip(parts, deltas[sub]))
                delta = jnp.sum(delta, axis=0, keepdims=True) * inverse
                stat_ref[h, 0:1, heres[sub]] = top + jnp.log2(total)
                stat_ref[h, 1:2, heres[sub]] = delta
                ready[sub] = [p * inverse for p in parts], delta

            def weigh(sub, u):
                mine = slice(sub * SUB, (sub + 1) * SUB)
                parts, delta = ready[sub]
                for i in range(u * UNIT, (u + 1) * UNIT, STRIP):
                    at = slice(i, i + STRIP)
                    to = slice(sub * SUB + i, sub * SUB + i + STRIP)
                    w = s_buf[sub, at] * parts[u]
                    w_buf[to, mine] = w.astype(jnp.bfloat16)
                    d_buf[to, mine] = (w * (p_buf[sub, at] - delta)).astype(jnp.bfloat16)

            def query_grad(sub):
                mine = slice(sub * SUB, (sub + 1) * SUB)
                span = slice(sub * SUB, sub * SUB + SPAN)
                flip = k_flip[:, rows_at(first + sub * SUB, SPAN) if tiles > 1 else span]
                dq = dot(flip, d_buf[span, mine], (1, 0))
                dq_all[heres[sub]] = (dq * SCALE).T.astype(jnp.bfloat16)

            def key_grads(sub):
                mine = slice(sub * SUB, (sub + 1) * SUB)
                for which, buf, right in ((0, d_buf, query[sub]), (1, w_buf, grad[sub])):
                    if tiles > 1:
                        spot = rows_at(first + sub * SUB, SPAN)
                        scratch[11][which, spot] += dot(
                            buf[sub * SUB:sub * SUB + SPAN, mine], right, (1, 0)
                        )
                        continue
                    own = dot(buf[HALF:HALF + TILE, mine], right, (1, 0))
                    near = dot(buf[HALF + TILE:SPAN + sub * SUB, mine], right, (1, 0))
                    if sub == 0:
                        part_ref[which, :, lanes] = own
                        n_buf[which] = near
                    else:
                        part_ref[which, :, lanes] += own
                        near0 = n_buf[which] + near[:SUB]
                        give_ref[which, :SUB, lanes] = near0.astype(jnp.bfloat16)
                        give_ref[which, SUB:, lanes] = near[SUB:].astype(jnp.bfloat16)

            every = range(UNITS)
            for sub in subs:
                for u in every:
                    score(sub, u)
                    product(sub, u)
            for sub in subs:
                settle(sub)
                for u in every:
                    weigh(sub, u)
            for sub in subs:
                query_grad(sub)
                key_grads(sub)

        if tiles > 1:
            pl.loop(0, tiles)(each_tile)
            part_ref[:, :, lanes] = scratch[11][:, HALF:HALF + rows]
            give_ref[:, :, lanes] = scratch[11][:, HALF + rows:].astype(jnp.bfloat16)
        else:
            each_tile(0)
        for k in range(n):
            dq_refs[k][:, lanes] = dq_all[rows_at(place_ref[k] * r, r)]

    over_heads(width // HEAD_DIM, refs[3:], each_head)


def query_part(place, halo, turn, kv, qd, far, near):
    n = len(kv)
    _, r, width = kv[0].shape
    rows = n * r
    heads = width // HEAD_DIM
    ext = rows + 2 * HALF
    here, scalars = pl.BlockSpec(memory_space=pltpu.VMEM), pl.BlockSpec(memory_space=pltpu.SMEM)
    scratch = [
        pltpu.VMEM((ext, HEAD_DIM), jnp.bfloat16),
        pltpu.VMEM((ext, HEAD_DIM), jnp.bfloat16),
        pltpu.VMEM((HEAD_DIM, ext), jnp.bfloat16),
        pltpu.VMEM((rows, HEAD_DIM), jnp.bfloat16),
        pltpu.VMEM((rows, HEAD_DIM), jnp.bfloat16),
        pltpu.VMEM((rows, HEAD_DIM), jnp.bfloat16),
        pltpu.VMEM((TILE // SUB, SPAN, SUB), jnp.float32),
        pltpu.VMEM((TILE // SUB, SPAN, SUB), jnp.float32),
        pltpu.VMEM((TILE + 2 * HALF, TILE), jnp.bfloat16),
        pltpu.VMEM((TILE + 2 * HALF, TILE), jnp.bfloat16),
        pltpu.VMEM((2, SUB, HEAD_DIM), jnp.float32),
    ]
    if rows != TILE:
        scratch.append(pltpu.VMEM((2, ext, HEAD_DIM), jnp.float32))
    scratch = [pltpu.VMEM((min(QGROUP, heads), *x.shape), x.dtype) for x in scratch]
    outs = pl.pallas_call(
        lambda *refs: query_kernel(n, len(far), *refs),
        in_specs=[scalars] * 3 + [here] * (n + 1 + 2 * len(far)),
        out_specs=[here] * (n + 3),
        scratch_shapes=scratch,
        out_shape=[jax.ShapeDtypeStruct((r, width), jnp.bfloat16)] * n
        + [
            jax.ShapeDtypeStruct((heads, 2, rows), jnp.float32),
            jax.ShapeDtypeStruct((2, rows, width), jnp.float32),
            jax.ShapeDtypeStruct((2, HALF, width), jnp.bfloat16),
        ],
        compiler_params=pltpu.CompilerParams(vmem_limit_bytes=VMEM_BYTES),
        cost_estimate=pl.CostEstimate(
            flops=10 * heads * rows * SPAN * HEAD_DIM,
            bytes_accessed=12 * rows * width,
            transcendentals=heads * rows * SPAN,
        ),
        name="query_part",
    )(place, halo, turn, *kv, qd, *far, *near)
    return outs[:n], outs[n], outs[n + 1], outs[n + 2]


def key_kernel(n, place_ref, halo_ref, turn_ref, *refs):
    kv_refs, refs = refs[:n], refs[n:]
    far_ref, stat_ref, part_ref, got_ref = refs[:4]
    out_refs = refs[4:4 + n]
    r, width = kv_refs[0].shape[1:]
    rows = n * r
    ahead = ahead_by(turn_ref)
    steps = HALF // SUB

    def each_head(h, scratch):
        k_all, v_all, q_all, g_all, low, w_buf, d_buf = scratch
        lanes = rows_at(h * HEAD_DIM, HEAD_DIM)
        for k in range(n):
            at = rows_at(place_ref[k] * r, r)
            k_all[at] = kv_refs[k][0, :, lanes]
            v_all[at] = kv_refs[k][1, :, lanes]
        for i in range(HALF // r):
            at = rows_at(halo_ref[i] * r, r)
            q_all[at] = far_ref[i, 0, :, lanes]
            g_all[at] = far_ref[i, 1, :, lanes]
        for b in range(steps):
            here = slice(b * SUB, (b + 1) * SUB)
            there = slice((steps - 1 - b) * SUB, (steps - b) * SUB)
            query, grad = q_all[here], g_all[here]
            log_total = jnp.where(turn_ref[1] > 0, stat_ref[h, 0:1, there], -NEG)
            delta = stat_ref[h, 1:2, there]
            for a in range(b + 1):
                at = slice(a * SUB, (a + 1) * SUB)
                w = jnp.exp2(dot(k_all[at], query, (1, 1)) * RATE - log_total)
                if a == b:
                    w = jnp.where(ahead <= 0, w, 0.0)
                w_buf[at, here] = w.astype(jnp.bfloat16)
                ds = w * (dot(v_all[at], grad, (1, 1)) - delta)
                d_buf[at, here] = ds.astype(jnp.bfloat16)
        for which, buf, right in ((0, d_buf, q_all), (1, w_buf, g_all)):
            for a in range(rows // SUB):
                at = slice(a * SUB, (a + 1) * SUB)
                value = part_ref[which, at, lanes]
                if a < steps:
                    value += dot(buf[at, a * SUB:], right[a * SUB:], (1, 0))
                if a >= rows // SUB - steps:
                    first = (rows // SUB - 1 - a) * SUB
                    value += got_ref[which, first:first + SUB, lanes].astype(jnp.float32)
                if which == 0:
                    value = value * SCALE
                low[which, at] = value.astype(jnp.bfloat16)
        for k in range(n):
            at = rows_at(place_ref[k] * r, r)
            out_refs[k][:, :, lanes] = low[:, at]

    over_heads(width // HEAD_DIM, refs[4 + n:], each_head)


def key_part(place, halo, turn, kv, far, stat, part, got):
    n = len(kv)
    _, r, width = kv[0].shape
    rows = n * r
    heads = width // HEAD_DIM
    here, scalars = pl.BlockSpec(memory_space=pltpu.VMEM), pl.BlockSpec(memory_space=pltpu.SMEM)
    scratch = [
        pltpu.VMEM((rows, HEAD_DIM), jnp.bfloat16),
        pltpu.VMEM((rows, HEAD_DIM), jnp.bfloat16),
        pltpu.VMEM((HALF, HEAD_DIM), jnp.bfloat16),
        pltpu.VMEM((HALF, HEAD_DIM), jnp.bfloat16),
        pltpu.VMEM((2, rows, HEAD_DIM), jnp.bfloat16),
        pltpu.VMEM((HALF, HALF), jnp.bfloat16),
        pltpu.VMEM((HALF, HALF), jnp.bfloat16),
    ]
    return pl.pallas_call(
        lambda *refs: key_kernel(n, *refs),
        in_specs=[scalars] * 3 + [here] * (n + 4),
        out_specs=[here] * n,
        scratch_shapes=[pltpu.VMEM((min(KGROUP, heads), *x.shape), x.dtype) for x in scratch],
        out_shape=[jax.ShapeDtypeStruct((2, r, width), jnp.bfloat16)] * n,
        compiler_params=pltpu.CompilerParams(vmem_limit_bytes=VMEM_BYTES),
        cost_estimate=pl.CostEstimate(
            flops=HINT,
            bytes_accessed=24 * rows * width,
            transcendentals=heads * HALF * (HALF // 2 + SUB // 2),
        ),
        name="key_part",
    )(place, halo, turn, *kv, far, stat, part, got)


def swapped(array, first, idle=False):
    count, n = lax.axis_size("blk"), lax.axis_size("head")
    pairs = []
    for h in range(n):
        for b in range(count):
            other = b + 1 if b % 2 == first else b - 1
            if 0 <= other < count:
                pairs.append((h * count + b, h * count + other))
            elif idle:
                pairs.append((h * count + b, (h ^ 1) * count + b))
    return lax.ppermute(array, ("head", "blk"), pairs)


def exchanged(pieces):
    n = len(pieces)
    moved = {
        k: lax.ppermute(pieces[k], "head", [(i, i ^ k) for i in range(n)])
        for k in range(1, n)
    }
    return [pieces[0]] + [moved[k] for k in range(1, n)]


def shards(query, key_in, value, grad_out):
    n = lax.axis_size("head")
    blocks = HALF // query.shape[0]
    index = lax.axis_index("blk").astype(jnp.int32)
    odd = index & 1
    order = lax.axis_index("head").astype(jnp.int32) ^ jnp.arange(n, dtype=jnp.int32)
    place = order ^ (odd * (n - 2))
    if n == blocks:
        halo = place
    else:
        halo = jnp.arange(blocks, dtype=jnp.int32) ^ (blocks - 2)
    has_far = jnp.logical_and(index > 0, index < lax.axis_size("blk") - 1)
    turn = jnp.stack([1 - 2 * odd, has_far.astype(jnp.int32)])

    kv = exchanged(packed(n, key_in, value))
    qd = exchanged(packed(n, query, grad_out))
    if n == blocks:
        groups = [stacked(kv[:-1]), kv[-1][None]]
        kv_far = [swapped(groups[0], 1), swapped(groups[1], 1, True)]
        kv_near = [swapped(group, 0) for group in groups]
        qd = stacked(qd, HINT)
        qd_far = swapped(qd, 1, True)
        key_halo = place
    else:
        local, qd = jnp.stack(kv), jnp.stack(qd)
        local = jnp.take(local, place, axis=0)
        kv_far = [swapped(local[:blocks], 1)]
        kv_near = [swapped(local[n - blocks:], 0)]
        qd_far = swapped(jnp.take(qd, place[:blocks], axis=0), 1, True)
        key_halo = halo
    dq, stat, part, give = query_part(place, halo, turn, kv, qd, kv_far, kv_near)
    stat_far = swapped(stat[:, :, :HALF], 1, True)
    got = swapped(give, 0)
    dkv = key_part(place, key_halo, turn, kv, qd_far, stat_far, part, got)
    return *merged(exchanged(dq), HINT), *merged(exchanged(dkv))


def solution(mesh):
    spec = P(("blk", "head"), None)
    return jax.shard_map(
        shards, mesh=mesh, in_specs=(spec,) * 4, out_specs=(spec,) * 3, check_vma=False
    )
```

```python
import math

import jax
import jax.numpy as jnp
from jax import lax
from jax.experimental import pallas as pl
from jax.experimental.pallas import tpu as pltpu
from jax.sharding import PartitionSpec as P

HEADS = 16
HEAD_DIM = 128
HALF = 512
TILE = 512
SUB = 256
SPAN = SUB + 2 * HALF
CHUNKS = SPAN // SUB
NEG = -1e30
HINT = 30_000_000_000
STRIP = 64
UNIT = 128
UNITS = SPAN // UNIT
SCALE = HEAD_DIM ** -0.5
RATE = SCALE * math.log2(math.e)
VMEM_BYTES = 46 * 1024 * 1024
QGROUP = 4
KGROUP = 2
SMALL_BYTES = 8 * 1024 * 1024


def dot(a, b, contract):
    return lax.dot_general(
        a, b, ((contract[:1], contract[1:]), ((), ())), preferred_element_type=jnp.float32
    )


def rows_at(start, size):
    return pl.ds(pl.multiple_of(start, size), size)


def pack_kernel(*refs):
    ins, outs, sems = refs[:2], refs[2:-1], refs[-1]
    n = len(outs)
    width = outs[0].shape[2]
    me = lax.axis_index("head")
    copies = []
    for k, out in enumerate(outs):
        columns = pl.ds(pl.multiple_of((me ^ k) * width, 128), width)
        for which in range(2):
            copies.append(
                pltpu.make_async_copy(ins[which].at[:, columns], out.at[which], sems.at[2 * k + which])
            )
    for copy in copies:
        copy.start()
    for copy in copies:
        copy.wait()


def packed(n, first, second):
    r, width = first.shape[0], first.shape[1] // n
    return pl.pallas_call(
        pack_kernel,
        in_specs=[pl.BlockSpec(memory_space=pltpu.HBM)] * 2,
        out_specs=[pl.BlockSpec(memory_space=pltpu.VMEM)] * n,
        out_shape=[jax.ShapeDtypeStruct((2, r, width), first.dtype)] * n,
        scratch_shapes=[pltpu.SemaphoreType.DMA((2 * n,))],
        compiler_params=pltpu.CompilerParams(vmem_limit_bytes=SMALL_BYTES),
        name="pack",
    )(first, second)


def stack_kernel(*refs):
    n = (len(refs) - 2)
    ins, out, sems = refs[:n], refs[n], refs[n + 1]
    copies = [pltpu.make_async_copy(ins[k], out.at[k], sems.at[k]) for k in range(n)]
    for copy in copies:
        copy.start()
    for copy in copies:
        copy.wait()


def stacked(pieces, flops=0):
    n = len(pieces)
    return pl.pallas_call(
        stack_kernel,
        in_specs=[pl.BlockSpec(memory_space=pltpu.VMEM)] * n,
        out_specs=pl.BlockSpec(memory_space=pltpu.VMEM),
        out_shape=jax.ShapeDtypeStruct((n, *pieces[0].shape), pieces[0].dtype),
        scratch_shapes=[pltpu.SemaphoreType.DMA((n,))],
        compiler_params=pltpu.CompilerParams(vmem_limit_bytes=SMALL_BYTES),
        cost_estimate=pl.CostEstimate(flops=flops, bytes_accessed=0, transcendentals=0),
        name="stack",
    )(*pieces)


def merge_kernel(n, *refs):
    ins, outs, sems = refs[:n], refs[n:-1], refs[-1]
    width = ins[0].shape[-1]
    me = lax.axis_index("head")
    copies = []
    for k in range(n):
        columns = pl.ds(pl.multiple_of((me ^ k) * width, 128), width)
        for which, out in enumerate(outs):
            source = ins[k] if len(outs) == 1 else ins[k].at[which]
            copies.append(
                pltpu.make_async_copy(source, out.at[:, columns], sems.at[len(outs) * k + which])
            )
    for copy in copies:
        copy.start()
    for copy in copies:
        copy.wait()


def merged(pieces, flops=0):
    n = len(pieces)
    r, width = pieces[0].shape[-2:]
    count = 1 if pieces[0].ndim == 2 else 2
    return pl.pallas_call(
        lambda *refs: merge_kernel(n, *refs),
        in_specs=[pl.BlockSpec(memory_space=pltpu.VMEM)] * n,
        out_specs=[pl.BlockSpec(memory_space=pl.ANY)] * count,
        out_shape=[jax.ShapeDtypeStruct((r, n * width), pieces[0].dtype)] * count,
        scratch_shapes=[pltpu.SemaphoreType.DMA((count * n,))],
        compiler_params=pltpu.CompilerParams(vmem_limit_bytes=SMALL_BYTES),
        cost_estimate=pl.CostEstimate(flops=flops, bytes_accessed=0, transcendentals=0),
        name="merge",
    )(*pieces)


def merge_pair_kernel(n, *refs):
    outs, sems = refs[-3:-1], refs[-1]
    batches = len(refs[:-3]) // n
    width = refs[0].shape[-1]
    me = lax.axis_index("head")
    copies = []
    for b in range(batches):
        for k in range(n):
            start = ((me ^ k) * batches + b) * width
            columns = pl.ds(pl.multiple_of(start, 128), width)
            for which, out in enumerate(outs):
                source, sem = refs[b * n + k].at[which], sems.at[2 * (b * n + k) + which]
                copies.append(pltpu.make_async_copy(source, out.at[:, columns], sem))
    for copy in copies:
        copy.start()
    for copy in copies:
        copy.wait()


def merged_pair(batches):
    n = len(batches[0])
    r, width = batches[0][0].shape[-2:]
    pieces = [piece for batch in batches for piece in batch]
    return pl.pallas_call(
        lambda *refs: merge_pair_kernel(n, *refs),
        in_specs=[pl.BlockSpec(memory_space=pltpu.VMEM)] * len(pieces),
        out_specs=[pl.BlockSpec(memory_space=pl.ANY)] * 2,
        out_shape=[jax.ShapeDtypeStruct((r, len(pieces) * width), pieces[0].dtype)] * 2,
        scratch_shapes=[pltpu.SemaphoreType.DMA((2 * len(pieces),))],
        compiler_params=pltpu.CompilerParams(vmem_limit_bytes=SMALL_BYTES),
        name="merge",
    )(*pieces)


def ahead_by(turn_ref):
    return (
        lax.broadcasted_iota(jnp.int32, (SUB, SUB), 0)
        - lax.broadcasted_iota(jnp.int32, (SUB, SUB), 1)
    ) * turn_ref[0]


def over_heads(heads, scratch, each_head):
    group = scratch[0].shape[0]

    def each_group(i, _):
        for member in range(group):
            each_head(i * group + member, [ref.at[member] for ref in scratch])
        return 0

    lax.fori_loop(0, heads // group, each_group, 0)


def members(refs):
    return [ref.at[i] for ref in refs for i in range(ref.shape[0])]


def query_kernel(n, groups, place_ref, halo_ref, turn_ref, *refs):
    kv_refs, refs = refs[:n], refs[n:]
    qd_ref, refs = refs[0], refs[1:]
    far_refs, near_refs, refs = refs[:groups], refs[groups:2 * groups], refs[2 * groups:]
    dq_refs, refs = refs[:n], refs[n:]
    stat_ref, part_ref, give_ref = refs[:3]
    r, width = kv_refs[0].shape[1:]
    rows = n * r
    tiles = rows // TILE
    ahead = ahead_by(turn_ref)

    def each_head(h, scratch):
        k_ext, v_ext, k_flip, q_all, g_all, dq_all = scratch[:6]
        s_buf, p_buf, w_buf, d_buf, n_buf = scratch[6:11]
        lanes = rows_at(h * HEAD_DIM, HEAD_DIM)
        for i, (far, near) in enumerate(zip(members(far_refs), members(near_refs))):
            at = halo_ref[i] * r
            for which, ext in ((0, k_ext), (1, v_ext)):
                ext[rows_at(at, r)] = far[which, :, lanes]
                ext[rows_at(HALF + rows + at, r)] = near[which, :, lanes]
        for k in range(n):
            at = place_ref[k] * r
            for which, ext in ((0, k_ext), (1, v_ext)):
                ext[rows_at(HALF + at, r)] = kv_refs[k][which, :, lanes]
            q_all[rows_at(at, r)] = qd_ref[k, 0, :, lanes]
            g_all[rows_at(at, r)] = qd_ref[k, 1, :, lanes]
        k_flip[...] = k_ext[...].T
        if tiles > 1:
            scratch[11][...] = jnp.zeros_like(scratch[11])

        def each_tile(tile):
            first = tile * TILE
            has_far = turn_ref[1] > 0
            if tiles > 1:
                has_far = jnp.logical_or(has_far, tile > 0)

            subs = range(TILE // SUB)
            heres = [rows_at(first + sub * SUB, SUB) for sub in subs]
            query = [q_all[here] for here in heres]
            grad = [g_all[here] for here in heres]
            tops = [[] for _ in subs]
            totals = [[] for _ in subs]
            deltas = [[] for _ in subs]
            ready = {}

            def folded(x, op):
                return op(x.reshape(x.shape[0] // 8, 8, SUB), axis=0)

            def score(sub, u):
                keys = rows_at(first + sub * SUB + u * UNIT, UNIT)
                s = dot(k_ext[keys], query[sub], (1, 1)) * RATE
                keep = None
                c = u * UNIT // SUB
                inside = slice(u * UNIT % SUB, u * UNIT % SUB + UNIT)
                if c == 0:
                    keep = ahead[inside] >= 0
                if c == CHUNKS - 1:
                    keep = ahead[inside] <= 0
                if sub + c < HALF // SUB:
                    keep = has_far if keep is None else jnp.logical_and(keep, has_far)
                if keep is not None:
                    s = jnp.where(keep, s, NEG)
                top = jnp.max(folded(s, jnp.max), axis=0, keepdims=True)
                e = jnp.exp2(s - top)
                s_buf[sub, u * UNIT:(u + 1) * UNIT] = e
                tops[sub].append(top)
                totals[sub].append(folded(e, jnp.sum))

            def product(sub, u):
                keys = rows_at(first + sub * SUB + u * UNIT, UNIT)
                at = slice(u * UNIT, (u + 1) * UNIT)
                dp = dot(v_ext[keys], grad[sub], (1, 1))
                p_buf[sub, at] = dp
                deltas[sub].append(folded(s_buf[sub, at] * dp, jnp.sum))

            def settle(sub):
                top = tops[sub][0]
                for other in tops[sub][1:]:
                    top = jnp.maximum(top, other)
                parts = [jnp.exp2(other - top) for other in tops[sub]]
                total = sum(p * t for p, t in zip(parts, totals[sub]))
                total = jnp.sum(total, axis=0, keepdims=True)
                inverse = 1.0 / total
                delta = sum(p * d for p, d in zip(parts, deltas[sub]))
                delta = jnp.sum(delta, axis=0, keepdims=True) * inverse
                stat_ref[h, 0:1, heres[sub]] = top + jnp.log2(total)
                stat_ref[h, 1:2, heres[sub]] = delta
                ready[sub] = [p * inverse for p in parts], delta

            def weigh(sub, u):
                mine = slice(sub * SUB, (sub + 1) * SUB)
                parts, delta = ready[sub]
                for i in range(u * UNIT, (u + 1) * UNIT, STRIP):
                    at = slice(i, i + STRIP)
                    to = slice(sub * SUB + i, sub * SUB + i + STRIP)
                    w = s_buf[sub, at] * parts[u]
                    w_buf[to, mine] = w.astype(jnp.bfloat16)
                    d_buf[to, mine] = (w * (p_buf[sub, at] - delta)).astype(jnp.bfloat16)

            def query_grad(sub):
                mine = slice(sub * SUB, (sub + 1) * SUB)
                span = slice(sub * SUB, sub * SUB + SPAN)
                flip = k_flip[:, rows_at(first + sub * SUB, SPAN) if tiles > 1 else span]
                dq = dot(flip, d_buf[span, mine], (1, 0))
                dq_all[heres[sub]] = (dq * SCALE).T.astype(jnp.bfloat16)

            def key_grads(sub):
                mine = slice(sub * SUB, (sub + 1) * SUB)
                for which, buf, right in ((0, d_buf, query[sub]), (1, w_buf, grad[sub])):
                    if tiles > 1:
                        spot = rows_at(first + sub * SUB, SPAN)
                        scratch[11][which, spot] += dot(
                            buf[sub * SUB:sub * SUB + SPAN, mine], right, (1, 0)
                        )
                        continue
                    own = dot(buf[HALF:HALF + TILE, mine], right, (1, 0))
                    near = dot(buf[HALF + TILE:SPAN + sub * SUB, mine], right, (1, 0))
                    if sub == 0:
                        part_ref[which, :, lanes] = own
                        n_buf[which] = near
                    else:
                        part_ref[which, :, lanes] += own
                        near0 = n_buf[which] + near[:SUB]
                        give_ref[which, :SUB, lanes] = near0.astype(jnp.bfloat16)
                        give_ref[which, SUB:, lanes] = near[SUB:].astype(jnp.bfloat16)

            every = range(UNITS)
            for sub in subs:
                for u in every:
                    score(sub, u)
                    product(sub, u)
            for sub in subs:
                settle(sub)
                for u in every:
                    weigh(sub, u)
            for sub in subs:
                query_grad(sub)
                key_grads(sub)

        if tiles > 1:
            pl.loop(0, tiles)(each_tile)
            part_ref[:, :, lanes] = scratch[11][:, HALF:HALF + rows]
            give_ref[:, :, lanes] = scratch[11][:, HALF + rows:].astype(jnp.bfloat16)
        else:
            each_tile(0)
        for k in range(n):
            dq_refs[k][:, lanes] = dq_all[rows_at(place_ref[k] * r, r)]

    over_heads(width // HEAD_DIM, refs[3:], each_head)


def query_part(place, halo, turn, kv, qd, far, near):
    n = len(kv)
    _, r, width = kv[0].shape
    rows = n * r
    heads = width // HEAD_DIM
    ext = rows + 2 * HALF
    here, scalars = pl.BlockSpec(memory_space=pltpu.VMEM), pl.BlockSpec(memory_space=pltpu.SMEM)
    scratch = [
        pltpu.VMEM((ext, HEAD_DIM), jnp.bfloat16),
        pltpu.VMEM((ext, HEAD_DIM), jnp.bfloat16),
        pltpu.VMEM((HEAD_DIM, ext), jnp.bfloat16),
        pltpu.VMEM((rows, HEAD_DIM), jnp.bfloat16),
        pltpu.VMEM((rows, HEAD_DIM), jnp.bfloat16),
        pltpu.VMEM((rows, HEAD_DIM), jnp.bfloat16),
        pltpu.VMEM((TILE // SUB, SPAN, SUB), jnp.float32),
        pltpu.VMEM((TILE // SUB, SPAN, SUB), jnp.float32),
        pltpu.VMEM((TILE + 2 * HALF, TILE), jnp.bfloat16),
        pltpu.VMEM((TILE + 2 * HALF, TILE), jnp.bfloat16),
        pltpu.VMEM((2, SUB, HEAD_DIM), jnp.float32),
    ]
    if rows != TILE:
        scratch.append(pltpu.VMEM((2, ext, HEAD_DIM), jnp.float32))
    scratch = [pltpu.VMEM((min(QGROUP, heads), *x.shape), x.dtype) for x in scratch]
    outs = pl.pallas_call(
        lambda *refs: query_kernel(n, len(far), *refs),
        in_specs=[scalars] * 3 + [here] * (n + 1 + 2 * len(far)),
        out_specs=[here] * (n + 3),
        scratch_shapes=scratch,
        out_shape=[jax.ShapeDtypeStruct((r, width), jnp.bfloat16)] * n
        + [
            jax.ShapeDtypeStruct((heads, 2, rows), jnp.float32),
            jax.ShapeDtypeStruct((2, rows, width), jnp.float32),
            jax.ShapeDtypeStruct((2, HALF, width), jnp.bfloat16),
        ],
        compiler_params=pltpu.CompilerParams(vmem_limit_bytes=VMEM_BYTES),
        cost_estimate=pl.CostEstimate(
            flops=10 * heads * rows * SPAN * HEAD_DIM,
            bytes_accessed=12 * rows * width,
            transcendentals=heads * rows * SPAN,
        ),
        name="query_part",
    )(place, halo, turn, *kv, qd, *far, *near)
    return outs[:n], outs[n], outs[n + 1], outs[n + 2]


def key_kernel(n, begin, place_ref, halo_ref, turn_ref, *refs):
    kv_refs, refs = refs[:n], refs[n:]
    far_ref, stat_ref, part_ref, got_ref = refs[:4]
    out_refs = refs[4:4 + n]
    r, width = out_refs[0].shape[1:]
    rows = n * r
    ahead = ahead_by(turn_ref)
    steps = HALF // SUB

    def each_head(part, scratch):
        k_all, v_all, q_all, g_all, low, w_buf, d_buf = scratch
        h = begin + part
        lanes, out_lanes = rows_at(h * HEAD_DIM, HEAD_DIM), rows_at(part * HEAD_DIM, HEAD_DIM)
        for k in range(n):
            at = rows_at(place_ref[k] * r, r)
            k_all[at] = kv_refs[k][0, :, lanes]
            v_all[at] = kv_refs[k][1, :, lanes]
        for i in range(HALF // r):
            at = rows_at(halo_ref[i] * r, r)
            q_all[at] = far_ref[i, 0, :, lanes]
            g_all[at] = far_ref[i, 1, :, lanes]
        for b in range(steps):
            here = slice(b * SUB, (b + 1) * SUB)
            there = slice((steps - 1 - b) * SUB, (steps - b) * SUB)
            query, grad = q_all[here], g_all[here]
            log_total = jnp.where(turn_ref[1] > 0, stat_ref[h, 0:1, there], -NEG)
            delta = stat_ref[h, 1:2, there]
            for a in range(b + 1):
                at = slice(a * SUB, (a + 1) * SUB)
                w = jnp.exp2(dot(k_all[at], query, (1, 1)) * RATE - log_total)
                if a == b:
                    w = jnp.where(ahead <= 0, w, 0.0)
                w_buf[at, here] = w.astype(jnp.bfloat16)
                ds = w * (dot(v_all[at], grad, (1, 1)) - delta)
                d_buf[at, here] = ds.astype(jnp.bfloat16)
        for which, buf, right in ((0, d_buf, q_all), (1, w_buf, g_all)):
            for a in range(rows // SUB):
                at = slice(a * SUB, (a + 1) * SUB)
                value = part_ref[which, at, lanes]
                if a < steps:
                    value += dot(buf[at, a * SUB:], right[a * SUB:], (1, 0))
                if a >= rows // SUB - steps:
                    first = (rows // SUB - 1 - a) * SUB
                    value += got_ref[which, first:first + SUB, lanes].astype(jnp.float32)
                if which == 0:
                    value = value * SCALE
                low[which, at] = value.astype(jnp.bfloat16)
        for k in range(n):
            at = rows_at(place_ref[k] * r, r)
            out_refs[k][:, :, out_lanes] = low[:, at]

    over_heads(width // HEAD_DIM, refs[4 + n:], each_head)


def key_part(place, halo, turn, kv, far, stat, part, got, begin, heads):
    n = len(kv)
    _, r, width = kv[0].shape
    rows = n * r
    width = heads * HEAD_DIM
    here, scalars = pl.BlockSpec(memory_space=pltpu.VMEM), pl.BlockSpec(memory_space=pltpu.SMEM)
    scratch = [
        pltpu.VMEM((rows, HEAD_DIM), jnp.bfloat16),
        pltpu.VMEM((rows, HEAD_DIM), jnp.bfloat16),
        pltpu.VMEM((HALF, HEAD_DIM), jnp.bfloat16),
        pltpu.VMEM((HALF, HEAD_DIM), jnp.bfloat16),
        pltpu.VMEM((2, rows, HEAD_DIM), jnp.bfloat16),
        pltpu.VMEM((HALF, HALF), jnp.bfloat16),
        pltpu.VMEM((HALF, HALF), jnp.bfloat16),
    ]
    return pl.pallas_call(
        lambda *refs: key_kernel(n, begin, *refs),
        in_specs=[scalars] * 3 + [here] * (n + 4),
        out_specs=[here] * n,
        scratch_shapes=[pltpu.VMEM((min(KGROUP, heads), *x.shape), x.dtype) for x in scratch],
        out_shape=[jax.ShapeDtypeStruct((2, r, width), jnp.bfloat16)] * n,
        compiler_params=pltpu.CompilerParams(vmem_limit_bytes=VMEM_BYTES),
        cost_estimate=pl.CostEstimate(
            flops=HINT,
            bytes_accessed=24 * rows * width,
            transcendentals=heads * HALF * (HALF // 2 + SUB // 2),
        ),
        name="key_part",
    )(place, halo, turn, *kv, far, stat, part, got)


def swapped(array, first, idle=False):
    count, n = lax.axis_size("blk"), lax.axis_size("head")
    pairs = []
    for h in range(n):
        for b in range(count):
            other = b + 1 if b % 2 == first else b - 1
            if 0 <= other < count:
                pairs.append((h * count + b, h * count + other))
            elif idle:
                pairs.append((h * count + b, (h ^ 1) * count + b))
    return lax.ppermute(array, ("head", "blk"), pairs)


def exchanged(pieces):
    n = len(pieces)
    moved = {
        k: lax.ppermute(pieces[k], "head", [(i, i ^ k) for i in range(n)])
        for k in range(1, n)
    }
    return [pieces[0]] + [moved[k] for k in range(1, n)]


def shards(query, key_in, value, grad_out):
    n = lax.axis_size("head")
    blocks = HALF // query.shape[0]
    index = lax.axis_index("blk").astype(jnp.int32)
    odd = index & 1
    order = lax.axis_index("head").astype(jnp.int32) ^ jnp.arange(n, dtype=jnp.int32)
    place = order ^ (odd * (n - 2))
    if n == blocks:
        halo = place
    else:
        halo = jnp.arange(blocks, dtype=jnp.int32) ^ (blocks - 2)
    has_far = jnp.logical_and(index > 0, index < lax.axis_size("blk") - 1)
    turn = jnp.stack([1 - 2 * odd, has_far.astype(jnp.int32)])

    kv = exchanged(packed(n, key_in, value))
    qd = exchanged(packed(n, query, grad_out))
    if n == blocks:
        groups = [stacked(kv[:-1]), kv[-1][None]]
        kv_far = [swapped(groups[0], 1), swapped(groups[1], 1, True)]
        kv_near = [swapped(group, 0) for group in groups]
        qd = stacked(qd, HINT)
        qd_far = swapped(qd, 1, True)
        key_halo = place
    else:
        local, qd = jnp.stack(kv), jnp.stack(qd)
        local = jnp.take(local, place, axis=0)
        kv_far = [swapped(local[:blocks], 1)]
        kv_near = [swapped(local[n - blocks:], 0)]
        qd_far = swapped(jnp.take(qd, place[:blocks], axis=0), 1, True)
        key_halo = halo
    dq, stat, part, give = query_part(place, halo, turn, kv, qd, kv_far, kv_near)
    stat_far = swapped(stat[:, :, :HALF], 1, True)
    got = swapped(give, 0)
    heads = stat.shape[0]
    batch = max(1, heads // 2)
    dkv = [
        key_part(place, key_halo, turn, kv, qd_far, stat_far, part, got, begin, batch)
        for begin in range(0, heads, batch)
    ]
    return *merged(exchanged(dq), HINT), *merged_pair([exchanged(pieces) for pieces in dkv])


def solution(mesh):
    spec = P(("blk", "head"), None)
    return jax.shard_map(
        shards, mesh=mesh, in_specs=(spec,) * 4, out_specs=(spec,) * 3, check_vma=False
    )
```
